512 devices in a mesh: leaf: 64 (over x, z), front: 8 (over y, core).
Axes of the slice: x: 4, y: 4, z: 16, core: 2. Of those that a mesh axis runs over, the one named last changes fastest.
Arguments:
- basis: bfloat16 [16, 90112], P(None, ('leaf', 'front')), may hold values from -6 to 6
- order: int32 [64, 1408], P('leaf'), may hold values from 0 to 1407, each once within a row
- leaf_inverse: bfloat16 [65536, 1024], P(('leaf', 'front')), may hold values from -0.1875 to 0.1875
- leaf_upper_inverse: bfloat16 [65536, 1024], P(('leaf', 'front')), may hold values from -0.1875 to 0.1875
- leaf_coupling_low: bfloat16 [8192, 2048], P(('leaf', 'front')), may hold values from -0.0625 to 0.0625
- leaf_coupling_up: bfloat16 [65536, 256], P(('leaf', 'front')), may hold values from -0.1875 to 0.1875
- sep_lower_inverse: bfloat16 [8192, 1792], P(('leaf', 'front')), may hold values from -4 to 4
- sep_upper_inverse: bfloat16 [8192, 1792], P(('leaf', 'front')), may hold values from -4 to 4
- sep_coupling_low: bfloat16 [8192, 1536], P(('leaf', 'front')), may hold values from -4 to 4
- sep_coupling_up: bfloat16 [8192, 1536], P(('leaf', 'front')), may hold values from -4 to 4
Outputs:
- shifted: bfloat16 [16, 90112], P(None, ('leaf', 'front'))
The draws below stay inside these ranges and needn't reach their ends.
All inputs are finite; a program needn't handle non-finite values.
Results may differ from the reference program's by a relative error of at most 0.015.
Values may be sent and summed in bfloat16 or wider, within the bound.
No kernel may reach another device: no remote copies, remote signals or barrier semaphores. Data moves between devices by JAX's collectives and lax.ppermute only.
A program may use at most 64 MiB of HBM per device.

```python
import jax
import jax.numpy as jnp
from jax import lax

BLOCK = 16
SUB_DEV = 128
SEP_DEV = 16
LEVELS = 3
ROWS_DEV = 176
SECTION = 1024
GROUP = 1408
NROWS = 90112
SEPCOLS = 1792
COUPCOLS = 1536
N_LEAF = 64
N_FRONT = 8


def segment_scale(total_cols, offset, factor):
    column = jnp.arange(total_cols, dtype=jnp.int32) // (N_FRONT * SEP_DEV) + offset
    span_size = jnp.ones_like(column)
    for power_two in range(1, LEVELS + 2):
        span_size = jnp.where(column >= 2 ** power_two, 2 ** power_two, span_size)
    return factor / jnp.sqrt((span_size * N_FRONT * SEP_DEV).astype(jnp.float32))


def draw_sep_lower_inverse(key, part):
    key = jax.random.fold_in(key, 11)
    full_shape = (N_LEAF * N_FRONT * SEP_DEV, SEPCOLS)
    values = jnp.clip(jax.random.normal(key, full_shape, jnp.float32), -4.0, 4.0)
    return (values * segment_scale(SEPCOLS, 2, 1.0)[None, :]).astype(jnp.bfloat16)


def draw_sep_upper_inverse(key, part):
    key = jax.random.fold_in(key, 23)
    full_shape = (N_LEAF * N_FRONT * SEP_DEV, SEPCOLS)
    values = jnp.clip(jax.random.normal(key, full_shape, jnp.float32), -4.0, 4.0)
    return (values * segment_scale(SEPCOLS, 2, 1.0)[None, :]).astype(jnp.bfloat16)


def draw_sep_coupling_low(key, part):
    key = jax.random.fold_in(key, 37)
    full_shape = (N_LEAF * N_FRONT * SEP_DEV, COUPCOLS)
    values = jnp.clip(jax.random.normal(key, full_shape, jnp.float32), -4.0, 4.0)
    return (values * segment_scale(COUPCOLS, 4, 0.5)[None, :]).astype(jnp.bfloat16)


def draw_sep_coupling_up(key, part):
    key = jax.random.fold_in(key, 41)
    full_shape = (N_LEAF * N_FRONT * SEP_DEV, COUPCOLS)
    values = jnp.clip(jax.random.normal(key, full_shape, jnp.float32), -4.0, 4.0)
    return (values * segment_scale(COUPCOLS, 4, 0.5)[None, :]).astype(jnp.bfloat16)


def level_of(key, dims, cuts, low, top_value):
    level = 1.0
    for axis_at, blocks in cuts:
        steps = jax.random.uniform(jax.random.fold_in(jax.random.fold_in(key, 6), axis_at), (blocks,), jnp.float32, low / len(cuts), top_value / len(cuts))
        level = level * jnp.repeat(jnp.exp(steps), dims[axis_at] // blocks).reshape((-1,) + (1,) * (len(dims) - 1 - axis_at))
    return level


def normal_values(key, shape, scale, reach, shards=(), kind=jnp.bfloat16):
    array = scale * jax.random.normal(key, shape, jnp.float32)
    if shards:
        array = array * level_of(key, shape, shards, -0.22, 0.18)
    return jnp.clip(array, -reach, reach).astype(kind)


def setup_inputs(seed: int = 0) -> dict:
    keys = jax.random.split(jax.random.key(seed), 11)
    basis = normal_values(keys[0], (BLOCK, NROWS), 1.0, 6.0, ((1, 512),))
    order = jax.vmap(lambda own: jax.random.permutation(own, GROUP))(jax.random.split(keys[1], N_LEAF)).reshape((N_LEAF, GROUP)).astype(jnp.int32)
    leaf_inverse = normal_values(keys[2], (N_LEAF * SECTION, SECTION), SECTION ** -0.5, 0.1875, ((0, 512),))
    leaf_upper_inverse = normal_values(keys[3], (N_LEAF * SECTION, SECTION), SECTION ** -0.5, 0.1875, ((0, 512),))
    leaf_coupling_low = normal_values(keys[4], (N_LEAF * N_FRONT * SEP_DEV, 2 * SECTION), (8 * SECTION) ** -0.5, 0.0625, ((0, 512),))
    leaf_coupling_up = normal_values(keys[5], (N_LEAF * SECTION, 2 * N_FRONT * SEP_DEV), (8 * N_FRONT * SEP_DEV) ** -0.5, 0.1875, ((0, 512),))
    sep_lower_inverse = draw_sep_lower_inverse(jax.random.fold_in(keys[10], 71), 0)
    sep_upper_inverse = draw_sep_upper_inverse(jax.random.fold_in(keys[10], 71), 0)
    sep_coupling_low = draw_sep_coupling_low(jax.random.fold_in(keys[10], 71), 0)
    sep_coupling_up = draw_sep_coupling_up(jax.random.fold_in(keys[10], 71), 0)
    return dict(basis=basis, order=order, leaf_inverse=leaf_inverse, leaf_upper_inverse=leaf_upper_inverse, leaf_coupling_low=leaf_coupling_low, leaf_coupling_up=leaf_coupling_up, sep_lower_inverse=sep_lower_inverse, sep_upper_inverse=sep_upper_inverse, sep_coupling_low=sep_coupling_low, sep_coupling_up=sep_coupling_up)


def group_apply(matrices, vectors):
    def one_group(operands):
        return jnp.dot(operands[1], operands[0].T, preferred_element_type=jnp.float32)
    result = lax.map(one_group, (matrices, jnp.transpose(vectors, (1, 0, 2))))
    return jnp.transpose(result, (1, 0, 2))


def node_apply(matrix, vectors, col_start):
    node_count = vectors.shape[1]
    col_width = vectors.shape[2]
    total_rows = matrix.shape[0]
    blocks = matrix[:, col_start:col_start + col_width].reshape(node_count, total_rows // node_count, col_width)
    result = jnp.einsum("nic,bnc->bni", blocks.astype(jnp.float32), vectors.astype(jnp.float32))
    return result.reshape(vectors.shape[0], total_rows)


def reference(basis, order, leaf_inverse, leaf_upper_inverse, leaf_coupling_low, leaf_coupling_up, sep_lower_inverse, sep_upper_inverse, sep_coupling_low, sep_coupling_up):
    unit_cols = N_FRONT * SEP_DEV
    grouped = basis.reshape(BLOCK, N_LEAF, GROUP)
    ordered = jnp.take_along_axis(grouped, order[None, :, :], axis=2)
    slot_grid = ordered.reshape(BLOCK, N_LEAF, N_FRONT, ROWS_DEV)
    leaf_rhs = slot_grid[:, :, :, :SUB_DEV].reshape(BLOCK, N_LEAF, SECTION)
    leaf_out = group_apply(leaf_inverse.reshape(N_LEAF, SECTION, SECTION), leaf_rhs).astype(jnp.bfloat16)

    def own_rows(level_idx):
        slot_start = SUB_DEV + (level_idx - 1) * SEP_DEV
        return slot_grid[:, :, :, slot_start:slot_start + SEP_DEV].reshape(BLOCK, N_LEAF * unit_cols)

    forward = []
    for level_idx in range(1, LEVELS + 1):
        node_count = N_LEAF // 2 ** level_idx
        col_width = unit_cols * 2 ** level_idx
        if level_idx == 1:
            children = leaf_out.reshape(BLOCK, node_count, 2 * SECTION)
            coupled = node_apply(leaf_coupling_low, children, 0)
        else:
            children = forward[-1].reshape(BLOCK, node_count, col_width)
            coupled = node_apply(sep_coupling_low, children, unit_cols * (2 ** level_idx - 4))
        reduced = (own_rows(level_idx).astype(jnp.float32) - coupled).astype(jnp.bfloat16)
        solved_level = node_apply(sep_lower_inverse, reduced.reshape(BLOCK, node_count, col_width), unit_cols * (2 ** level_idx - 2))
        forward.append(solved_level.astype(jnp.bfloat16))

    backward = [None] * LEVELS
    for level_idx in range(LEVELS, 0, -1):
        node_count = N_LEAF // 2 ** level_idx
        col_width = unit_cols * 2 ** level_idx
        if level_idx < LEVELS:
            parent = backward[level_idx].reshape(BLOCK, node_count // 2, 2 * col_width)
            parent = jnp.repeat(parent, 2, axis=1)
            coupled = node_apply(sep_coupling_up, parent, unit_cols * (2 ** (level_idx + 1) - 4))
            carried = (forward[level_idx - 1].astype(jnp.float32) - coupled).astype(jnp.bfloat16)
        else:
            carried = forward[level_idx - 1]
        solved_level = node_apply(sep_upper_inverse, carried.reshape(BLOCK, node_count, col_width), unit_cols * (2 ** level_idx - 2))
        backward[level_idx - 1] = solved_level.astype(jnp.bfloat16)

    parent = jnp.repeat(backward[0].reshape(BLOCK, N_LEAF // 2, 2 * unit_cols), 2, axis=1)
    coupled = node_apply(leaf_coupling_up, parent, 0)
    leaf_rest = (leaf_out.reshape(BLOCK, N_LEAF * SECTION).astype(jnp.float32) - coupled).astype(jnp.bfloat16)
    leaf_final = group_apply(leaf_upper_inverse.reshape(N_LEAF, SECTION, SECTION), leaf_rest.reshape(BLOCK, N_LEAF, SECTION)).astype(jnp.bfloat16)

    pieces = [leaf_final.reshape(BLOCK, N_LEAF, N_FRONT, SUB_DEV)]
    for level_idx in range(LEVELS):
        pieces.append(backward[level_idx].reshape(BLOCK, N_LEAF, N_FRONT, SEP_DEV))
    solved = jnp.concatenate(pieces, axis=3).reshape(BLOCK, N_LEAF, GROUP)
    inverse = jnp.argsort(order, axis=1).astype(jnp.int32)
    restored = jnp.take_along_axis(solved, inverse[None, :, :], axis=2)
    return restored.reshape(BLOCK, NROWS)
```

```python
import jax
import jax.numpy as jnp
from jax import lax
from jax.sharding import Mesh, PartitionSpec as P

AXES = ("sub", "a", "b", "c", "front")
PAIR = ("c", "front")
PLANES4 = ("b", "c")
PLANES8 = ("a", "b", "c")
BF = jnp.bfloat16
WIDE = 256


def mm(x, w):
    return lax.dot_general(x, w, (((1,), (1,)), ((), ())), preferred_element_type=jnp.float32)


def exchange(x, axes):
    return lax.all_to_all(x, axes, 0, 0)


def spread(x, axes):
    size = lax.axis_size(axes)
    return exchange(jnp.broadcast_to(x[None], (size,) + x.shape), axes)


def total(parts):
    return jnp.sum(parts.astype(jnp.float32), axis=0)


def local(
    basis,
    order,
    leaf_inverse,
    leaf_upper_inverse,
    leaf_coupling_low,
    leaf_coupling_up,
    sep_lower_inverse,
    sep_upper_inverse,
    sep_coupling_low,
    sep_coupling_up,
):
    ia, ib, ic = (lax.axis_index(n) for n in ("a", "b", "c"))
    f = lax.axis_index("front")
    leaf = 4 * ia + 2 * ib + ic

    with jax.named_scope("gather_basis"):
        cols = jnp.pad(basis, ((0, 0), (0, WIDE - 176)))
        grouped = spread(cols, "front")

    with jax.named_scope("move_level1"):
        low = jnp.transpose(leaf_coupling_low.reshape(16, 16, 128), (1, 0, 2))
        a1 = jnp.broadcast_to(sep_lower_inverse[None, :, :256], (16, 16, 256))
        got = exchange(jnp.concatenate([low, a1], 2), PAIR)
        low_cols = got[:, :, :128].reshape(256, 128)
        a1 = got[:, :, 128:].reshape(256, 256)

    with jax.named_scope("move_level2"):
        g2 = jnp.transpose(sep_coupling_low[:, :512].reshape(16, 2, 256), (1, 0, 2))
        g2 = jnp.broadcast_to(g2[:, None], (2, 2, 16, 256)).reshape(4, 16, 256)
        a2 = jnp.broadcast_to(sep_lower_inverse[None, :, 256:768], (4, 16, 512))
        got = exchange(jnp.concatenate([g2, a2], 2), PLANES4)
        got = lax.all_gather(got, "front", axis=1).reshape(512, 768)
        g2 = got[:, :256]
        a2 = got[:, 256:]

    with jax.named_scope("move_level3"):
        g3 = jnp.transpose(sep_coupling_low[:, 512:].reshape(16, 2, 512), (1, 0, 2))
        g3 = jnp.broadcast_to(g3[:, None], (2, 4, 16, 512)).reshape(8, 16, 512)
        g3 = exchange(g3, PLANES8).reshape(128, 512)

        def by_front(m):
            return jnp.transpose(m.reshape(16, 8, 8, 16), (2, 0, 1, 3)).reshape(8, 16, 128)

        a3 = by_front(sep_lower_inverse[:, 768:])
        h2 = by_front(sep_coupling_up[:, 512:])
        up = jnp.transpose(leaf_upper_inverse.reshape(128, 8, 128), (1, 0, 2))
        got = exchange(jnp.concatenate([a3, h2, up], 1), "front")
        a3 = got[:, :16].reshape(128, 128)
        h2 = got[:, 16:32].reshape(128, 128)
        up = got[:, 32:].reshape(1024, 128)
        a3 = spread(a3, PLANES8).reshape(1024, 128)
        b3 = spread(sep_upper_inverse[:, 768:], PLANES8).reshape(128, 1024)
        h2 = spread(h2, PLANES4).reshape(512, 128)

    with jax.named_scope("move_down"):
        down = jnp.concatenate([sep_upper_inverse[:, :768], sep_coupling_up[:, :512]], 1)
        got = spread(down, PLANES4).reshape(2, 2, 16, 1280)
        mine = lax.dynamic_index_in_dim(got, ib, 0, keepdims=False)
        b2 = lax.all_gather(got[:, :, :, 256:768].reshape(4, 16, 512), "front", axis=1).reshape(512, 512)
        mine = jnp.concatenate([mine[:, :, :256], mine[:, :, 768:]], 2)
        mine = lax.all_gather(mine, "front", axis=1).reshape(256, 768)
        b1 = mine[:, :256]
        h1 = mine[:, 256:]

    with jax.named_scope("order"):
        place = (order[0] // 176) * WIDE + order[0] % 176
        slots = place.reshape(8, 176)
        leaf_place = slots[:, :128].reshape(1024)
        own_place = lax.dynamic_index_in_dim(slots, f, 0, keepdims=False)[128:]
        wide = 8 * WIDE
        hot = (leaf_place[:, None] == lax.broadcasted_iota(jnp.int32, (1024, wide), 1)).astype(BF)
        own_hot = (own_place[:, None] == lax.broadcasted_iota(jnp.int32, (48, wide), 1)).astype(BF)
        lower = lax.dot_general(leaf_inverse, hot, (((1,), (0,)), ((), ())), preferred_element_type=jnp.float32)
        lower = jnp.concatenate([lower.astype(BF), own_hot], 0)
        upper = lax.dot_general(hot, up, (((0,), (0,)), ((), ())), preferred_element_type=jnp.float32)
        upper = jnp.concatenate([upper.astype(BF), own_hot.T], 1)

    with jax.named_scope("weights1"):
        row = lax.broadcasted_iota(jnp.int32, (384, 48), 0)
        col = lax.broadcasted_iota(jnp.int32, (384, 48), 1)
        target = jnp.where(col < 16, (ic * 8 + f) * 16 + col, 240 + col)
        keep = (row == target).astype(BF)
        first = jnp.concatenate([jnp.pad(-low_cols, ((0, 128), (0, 0))), keep], 1)

    with jax.named_scope("leaf_lower"):
        grouped = jnp.transpose(grouped, (1, 0, 2)).reshape(16, wide)
        own = mm(grouped, lower).astype(BF)
        y_leaf = own[:, :128]

    with jax.named_scope("level1_up"):
        got = spread(mm(own, first).astype(BF), PAIR)
        c1 = total(got[:, :, :256]).astype(BF)
        rest = jnp.transpose(got[:, :, 256:288], (1, 0, 2))
        rhs2 = rest[:, :, :16].reshape(16, 256)
        rhs3 = lax.dynamic_index_in_dim(rest.reshape(16, 2, 8, 32)[:, :, :, 16:], f, 2, keepdims=False).reshape(16, 32)
        y1 = mm(c1, a1).astype(BF)

    with jax.named_scope("level2_up"):
        half = lax.broadcasted_iota(jnp.int32, (16, 512), 1) // 256
        part = jnp.where(half == ib, jnp.concatenate([rhs2, rhs2], 1).astype(jnp.float32), 0.0) - mm(y1, g2)
        part = jnp.concatenate([part.astype(BF), jnp.pad(rhs3, ((0, 0), (0, 96)))], 1)
        got = lax.all_gather(part, "b")
        c2 = total(got[:, :, :512]).astype(BF)
        rhs3 = jnp.transpose(got[:, :, 512:544], (1, 0, 2)).reshape(16, 64)
        y2 = mm(c2, a2).astype(BF)

    with jax.named_scope("level3_up"):
        half = lax.broadcasted_iota(jnp.int32, (16, 128), 1) // 64
        part = jnp.where(half == ia, jnp.concatenate([rhs3, rhs3], 1).astype(jnp.float32), 0.0) - mm(y2, g3)
        c3 = total(lax.all_gather(part.astype(BF), "a")).astype(BF)
        y3 = total(spread(mm(c3, a3).astype(BF), "front")).astype(BF)

    with jax.named_scope("level3_down"):
        z3 = mm(y3, b3).astype(BF)
        got = spread(mm(z3, h2).astype(BF), "front")
        w2 = (y2.astype(jnp.float32) - total(got)).astype(BF)

    with jax.named_scope("local_down"):
        z2 = mm(w2, b2).astype(BF)
        w1 = (y1.astype(jnp.float32) - mm(z2, h1)).astype(BF)
        z1 = mm(w1, b1).astype(BF)
        w_leaf = (y_leaf.astype(jnp.float32) - mm(z1, leaf_coupling_up)).astype(BF)
        own = jnp.concatenate(
            [
                w_leaf,
                lax.dynamic_slice_in_dim(z1, (ic * 8 + f) * 16, 16, 1),
                lax.dynamic_slice_in_dim(z2, ((2 * ib + ic) * 8 + f) * 16, 16, 1),
                lax.dynamic_slice_in_dim(z3, leaf * 16, 16, 1),
            ],
            1,
        )

    with jax.named_scope("leaf_upper"):
        out = mm(own, upper).astype(BF)
        out = jnp.transpose(out.reshape(16, 8, WIDE), (1, 0, 2))
        return total(exchange(out, "front"))[:, :176].astype(BF)


def solution(mesh):
    fronts = mesh.shape["front"]
    grid = Mesh(mesh.devices.reshape(-1, 2, 2, 2, fronts), AXES)
    rows = P(AXES, None)
    in_specs = (P(None, AXES), P(AXES[:4], None)) + (rows,) * 8
    return jax.shard_map(local, mesh=grid, in_specs=in_specs, out_specs=P(None, AXES), check_vma=False)
```

```python
import jax
import jax.numpy as jnp
from jax import lax
from jax.sharding import Mesh, PartitionSpec as P

AXES = ("sub", "a", "b", "c", "front")
PAIR = ("c", "front")
BF = jnp.bfloat16
WIDE = 256


def mm(x, w):
    return lax.dot_general(x, w, (((1,), (1,)), ((), ())), preferred_element_type=jnp.float32)


def exchange(x, axes):
    return lax.all_to_all(x, axes, 0, 0)


def spread(x, axes):
    size = lax.axis_size(axes)
    return exchange(jnp.broadcast_to(x[None], (size,) + x.shape), axes)


def total(parts):
    return jnp.sum(parts.astype(jnp.float32), axis=0)


def swap(x, axis):
    return lax.ppermute(x, axis, [(0, 1), (1, 0)])


def ordered(mine, other, index, at):
    low = jnp.where(index == 0, mine, other)
    high = jnp.where(index == 0, other, mine)
    return jnp.stack([low, high], at)


def columns(m, index, width):
    return lax.dynamic_slice_in_dim(m, index * width, width, 1)


def local(
    basis,
    order,
    leaf_inverse,
    leaf_upper_inverse,
    leaf_coupling_low,
    leaf_coupling_up,
    sep_lower_inverse,
    sep_upper_inverse,
    sep_coupling_low,
    sep_coupling_up,
):
    ia, ib, ic = (lax.axis_index(n) for n in ("a", "b", "c"))
    f = lax.axis_index("front")
    leaf = 4 * ia + 2 * ib + ic

    with jax.named_scope("first_exchange"):
        cols = jnp.pad(basis, ((0, 0), (0, WIDE - 176)))
        same = jnp.concatenate([cols, sep_lower_inverse[:, :256]], 1)
        low = jnp.transpose(leaf_coupling_low.reshape(16, 16, 128), (1, 0, 2))

        def by_front(m, groups):
            m = jnp.transpose(m.reshape(16, groups, 8, 16), (2, 0, 1, 3))
            return m.reshape(8, 16, groups * 16)

        moved = jnp.concatenate(
            [
                by_front(sep_lower_inverse[:, 768:], 8),
                by_front(sep_coupling_up[:, 512:], 8),
                jnp.pad(by_front(sep_lower_inverse[:, 256:768], 4), ((0, 0), (0, 0), (0, 64))),
            ],
            2,
        )
        moved = jnp.broadcast_to(moved[None], (2, 8, 16, 384)).reshape(16, 16, 384)
        same = jnp.broadcast_to(same[None], (16, 16, 512))
        got = exchange(jnp.concatenate([same, low, moved], 2), PAIR)
        grouped = lax.dynamic_slice_in_dim(got[:, :, :WIDE], ic * 8, 8, 0)
        a1 = got[:, :, 256:512].reshape(256, 256)
        low_cols = got[:, :, 512:640].reshape(256, 128)
        a3 = got[:, :, 640:768].reshape(2, 8, 16, 128)
        h2 = got[:, :, 768:896].reshape(2, 8, 16, 128)
        a2 = got[:, :, 896:960].reshape(2, 8, 16, 64)

    with jax.named_scope("planes_level2"):
        g2 = sep_coupling_low[:, :512]
        b2 = sep_upper_inverse[:, 256:768]
        mine = jnp.concatenate([columns(g2, ib, 256), b2], 1)
        other = swap(jnp.concatenate([columns(g2, 1 - ib, 256), b2], 1), "b")
        mine = ordered(mine, other, ib, 0).reshape(32, 768)
        down = jnp.concatenate([sep_coupling_up[:, :512], sep_upper_inverse[:, :256]], 1)
        mine = jnp.concatenate([mine, down], 0)
        other = swap(mine, "c")
        both = ordered(mine[:32].reshape(2, 16, 768), other[:32].reshape(2, 16, 768), ic, 1).reshape(64, 768)
        down = ordered(mine[32:], other[32:], ic, 0).reshape(32, 768)
        g2 = both[:, :256]
        b2 = both[:, 256:]

    with jax.named_scope("planes_level3"):
        g3 = sep_coupling_low[:, 512:]
        b3 = sep_upper_inverse[:, 768:]
        mine = jnp.concatenate([columns(g3, ia, 512), b3], 1)
        other = swap(jnp.concatenate([columns(g3, 1 - ia, 512), b3], 1), "a")
        mine = ordered(mine, other, ia, 0)
        mine = ordered(mine, swap(mine, "b"), ib, 1)
        mine = ordered(mine, swap(mine, "c"), ic, 2).reshape(128, 1536)
        g3 = mine[:, :512]
        b3 = mine[:, 512:]

    with jax.named_scope("planes_columns"):
        mine = jnp.concatenate([a2, jnp.zeros_like(a2), h2], 3)
        mine = ordered(mine, swap(mine, "b"), ib, 0).reshape(512, 256)
        a2 = mine[:, :64]
        h2 = mine[:, 128:]
        a3 = ordered(a3, swap(a3, "a"), ia, 0)
        a3 = ordered(a3, swap(a3, "b"), ib, 1).reshape(1024, 128)

    with jax.named_scope("gather_down"):
        tail = jnp.concatenate([down[:, :512], jnp.pad(down[:, 512:], ((0, 0), (0, 256)))], 0)
        tail = jnp.concatenate([b2, tail], 1)
        got = lax.all_gather(jnp.concatenate([leaf_upper_inverse, tail], 0), "front")
        up = lax.dynamic_slice_in_dim(got[:, :128], f * 128, 128, 2).reshape(1024, 128)
        b2 = jnp.transpose(got[:, 128:, :512].reshape(8, 4, 16, 512), (1, 0, 2, 3)).reshape(512, 512)
        h1 = jnp.transpose(got[:, 128:160, 512:].reshape(8, 2, 16, 512), (1, 0, 2, 3)).reshape(256, 512)
        b1 = jnp.transpose(got[:, 160:, 512:768].reshape(8, 2, 16, 256), (1, 0, 2, 3)).reshape(256, 256)

    with jax.named_scope("order"):
        place = (order[0] // 176) * WIDE + order[0] % 176
        slots = place.reshape(8, 176)
        leaf_place = slots[:, :128].reshape(1024)
        own_place = lax.dynamic_index_in_dim(slots, f, 0, keepdims=False)[128:]
        wide = 8 * WIDE
        hot = (leaf_place[:, None] == lax.broadcasted_iota(jnp.int32, (1024, wide), 1)).astype(BF)
        own_hot = (own_place[:, None] == lax.broadcasted_iota(jnp.int32, (48, wide), 1)).astype(BF)
        lower = lax.dot_general(leaf_inverse, hot, (((1,), (0,)), ((), ())), preferred_element_type=jnp.float32)
        lower = jnp.concatenate([lower.astype(BF), own_hot], 0)
        upper = lax.dot_general(hot, up, (((0,), (0,)), ((), ())), preferred_element_type=jnp.float32)
        upper = jnp.concatenate([upper.astype(BF), own_hot.T], 1)

    with jax.named_scope("weights1"):
        row = lax.broadcasted_iota(jnp.int32, (384, 48), 0)
        col = lax.broadcasted_iota(jnp.int32, (384, 48), 1)
        target = jnp.where(col < 16, (ic * 8 + f) * 16 + col, 240 + col)
        keep = (row == target).astype(BF)
        first = jnp.concatenate([jnp.pad(-low_cols, ((0, 128), (0, 0))), keep], 1)

    with jax.named_scope("leaf_lower"):
        grouped = jnp.transpose(grouped, (1, 0, 2)).reshape(16, wide)
        own = mm(grouped, lower).astype(BF)
        y_leaf = own[:, :128]

    with jax.named_scope("level1_up"):
        got = spread(mm(own, first).astype(BF), PAIR)
        c1 = total(got[:, :, :256]).astype(BF)
        rest = lax.dynamic_index_in_dim(got[:, :, 256:288].reshape(2, 8, 16, 32), f, 1, keepdims=False)
        rhs2 = jnp.transpose(rest[:, :, :16], (1, 0, 2)).reshape(16, 32)
        rhs3 = jnp.transpose(rest[:, :, 16:], (1, 0, 2)).reshape(16, 32)
        y1 = mm(c1, a1).astype(BF)

    with jax.named_scope("level2_up"):
        half = lax.broadcasted_iota(jnp.int32, (16, 64), 1) // 32
        part = jnp.where(half == ib, jnp.concatenate([rhs2, rhs2], 1).astype(jnp.float32), 0.0) - mm(y1, g2)
        part = jnp.concatenate([part.astype(BF), jnp.pad(rhs3, ((0, 0), (0, 32)))], 1)
        got = lax.all_gather(part, "b")
        c2 = total(got[:, :, :64]).astype(BF)
        rhs3 = jnp.transpose(got[:, :, 64:96], (1, 0, 2)).reshape(16, 64)
        y2 = total(spread(mm(c2, a2).astype(BF), "front")).astype(BF)

    with jax.named_scope("level3_up"):
        half = lax.broadcasted_iota(jnp.int32, (16, 128), 1) // 64
        part = jnp.where(half == ia, jnp.concatenate([rhs3, rhs3], 1).astype(jnp.float32), 0.0) - mm(y2, g3)
        c3 = total(lax.all_gather(part.astype(BF), "a")).astype(BF)
        y3 = total(spread(mm(c3, a3).astype(BF), "front")).astype(BF)

    with jax.named_scope("level3_down"):
        z3 = mm(y3, b3).astype(BF)
        got = spread(mm(z3, h2).astype(BF), "front")
        w2 = (y2.astype(jnp.float32) - total(got)).astype(BF)

    with jax.named_scope("local_down"):
        z2 = mm(w2, b2).astype(BF)
        w1 = (y1.astype(jnp.float32) - mm(z2, h1)).astype(BF)
        z1 = mm(w1, b1).astype(BF)
        w_leaf = (y_leaf.astype(jnp.float32) - mm(z1, leaf_coupling_up)).astype(BF)
        own = jnp.concatenate(
            [
                w_leaf,
                columns(z1, ic * 8 + f, 16),
                columns(z2, (2 * ib + ic) * 8 + f, 16),
                columns(z3, leaf, 16),
            ],
            1,
        )

    with jax.named_scope("leaf_upper"):
        out = mm(own, upper).astype(BF)
        out = jnp.transpose(out.reshape(16, 8, WIDE), (1, 0, 2))
        return total(exchange(out, "front"))[:, :176].astype(BF)


def solution(mesh):
    fronts = mesh.shape["front"]
    grid = Mesh(mesh.devices.reshape(-1, 2, 2, 2, fronts), AXES)
    rows = P(AXES, None)
    in_specs = (P(None, AXES), P(AXES[:4], None)) + (rows,) * 8
    return jax.shard_map(local, mesh=grid, in_specs=in_specs, out_specs=P(None, AXES), check_vma=False)
```

```python
import jax
import jax.numpy as jnp
from jax import lax
from jax.sharding import Mesh, PartitionSpec as P

AXES = ("sub", "a", "b", "c", "front")
PAIR = ("c", "front")
BF = jnp.bfloat16
WIDE = 256


def mm(x, w):
    return lax.dot_general(x, w, (((1,), (1,)), ((), ())), preferred_element_type=jnp.float32)


def exchange(x, axes):
    return lax.all_to_all(x, axes, 0, 0)


def spread(x, axes):
    size = lax.axis_size(axes)
    return exchange(jnp.broadcast_to(x[None], (size,) + x.shape), axes)


def total(parts):
    return jnp.sum(parts.astype(jnp.float32), axis=0)


def swap(x, axis):
    return lax.ppermute(x, axis, [(0, 1), (1, 0)])


def ordered(mine, other, index, at):
    low = jnp.where(index == 0, mine, other)
    high = jnp.where(index == 0, other, mine)
    return jnp.stack([low, high], at)


def columns(m, index, width):
    return lax.dynamic_slice_in_dim(m, index * width, width, 1)


def local(
    basis,
    order,
    leaf_inverse,
    leaf_upper_inverse,
    leaf_coupling_low,
    leaf_coupling_up,
    sep_lower_inverse,
    sep_upper_inverse,
    sep_coupling_low,
    sep_coupling_up,
):
    ia, ib, ic = (lax.axis_index(n) for n in ("a", "b", "c"))
    f = lax.axis_index("front")
    leaf = 4 * ia + 2 * ib + ic

    with jax.named_scope("first_exchange"):

        def by_front(m, groups):
            m = jnp.transpose(m.reshape(16, groups, 8, 16), (2, 0, 1, 3))
            return m.reshape(8, 16, groups * 16)

        def per_front(m):
            return jnp.broadcast_to(m[None], (2,) + m.shape).reshape((16,) + m.shape[1:])

        def for_all(m):
            return jnp.broadcast_to(m[None], (16,) + m.shape)

        low = jnp.transpose(leaf_coupling_low.reshape(16, 16, 128), (1, 0, 2))
        moved = jnp.concatenate(
            [
                for_all(jnp.pad(basis, ((0, 0), (0, 16)))),
                per_front(by_front(sep_lower_inverse[:, 256:768], 4)),
                for_all(sep_lower_inverse[:, :256]),
                for_all(sep_upper_inverse[:, :256]),
                low,
                per_front(by_front(sep_lower_inverse[:, 768:], 8)),
                per_front(by_front(sep_coupling_up[:, 512:], 8)),
                per_front(by_front(sep_coupling_up[:, :512], 4)),
                jnp.zeros((16, 16, 64), BF),
            ],
            2,
        )
        got = exchange(moved, PAIR)

    with jax.named_scope("planes_level2"):
        g2 = sep_coupling_low[:, :512]
        b2 = sep_upper_inverse[:, 256:768]
        level2 = jnp.concatenate([columns(g2, ib, 256), b2], 1)
        other = swap(jnp.concatenate([columns(g2, 1 - ib, 256), b2], 1), "b")
        level2 = ordered(level2, other, ib, 0)
        other = swap(level2, "c")

    with jax.named_scope("planes_level3"):
        g3 = sep_coupling_low[:, 512:]
        b3 = sep_upper_inverse[:, 768:]
        level3 = jnp.concatenate([columns(g3, ia, 512), b3], 1)
        other3 = swap(jnp.concatenate([columns(g3, 1 - ia, 512), b3], 1), "a")

    got, level2, other, level3, other3 = lax.optimization_barrier((got, level2, other, level3, other3))

    with jax.named_scope("unpack"):
        grouped = lax.dynamic_slice_in_dim(got[:, :, :WIDE], ic * 8, 8, 0)
        a2 = got[:, :, 192:256]
        a1 = got[:, :, 256:512].reshape(256, 256)
        b1 = got[:, :, 512:768].reshape(256, 256)
        low_cols = got[:, :, 768:896].reshape(256, 128)
        a3 = got[:, :, 896:1024]
        h2 = got[:, :, 1024:1152]
        h1 = got[:, :, 1152:1216].reshape(256, 64)
        level2 = ordered(level2, other, ic, 1).reshape(64, 768)
        g2 = level2[:, :256]
        b2 = level2[:, 256:]
        level3 = ordered(level3, other3, ia, 0)
        mixed = jnp.concatenate([a2, jnp.zeros_like(a2), h2], 2).reshape(256, 256)
        a3 = a3.reshape(256, 128)

    with jax.named_scope("planes_middle"):
        mixed_other = swap(mixed, "b")
        a3_other = swap(a3, "a")
        level3_other = swap(level3, "b")

    with jax.named_scope("order"):
        place = (order[0] // 176) * WIDE + order[0] % 176
        slots = place.reshape(8, 176)
        leaf_place = slots[:, :128].reshape(1024)
        own_place = lax.dynamic_index_in_dim(slots, f, 0, keepdims=False)[128:]
        wide = 8 * WIDE
        hot = (leaf_place[:, None] == lax.broadcasted_iota(jnp.int32, (1024, wide), 1)).astype(BF)
        own_hot = (own_place[:, None] == lax.broadcasted_iota(jnp.int32, (48, wide), 1)).astype(BF)
        lower = lax.dot_general(leaf_inverse, hot, (((1,), (0,)), ((), ())), preferred_element_type=jnp.float32)
        lower = jnp.concatenate([lower.astype(BF), own_hot], 0)

    with jax.named_scope("weights1"):
        row = lax.broadcasted_iota(jnp.int32, (384, 48), 0)
        col = lax.broadcasted_iota(jnp.int32, (384, 48), 1)
        target = jnp.where(col < 16, (ic * 8 + f) * 16 + col, 240 + col)
        keep = (row == target).astype(BF)
        first = jnp.concatenate([jnp.pad(-low_cols, ((0, 128), (0, 0))), keep], 1)

    with jax.named_scope("leaf_lower"):
        grouped = jnp.transpose(grouped, (1, 0, 2)).reshape(16, wide)
        own = mm(grouped, lower).astype(BF)
        y_leaf = own[:, :128]

    with jax.named_scope("level1_up"):
        got = spread(mm(own, first).astype(BF), PAIR)
        c1 = total(got[:, :, :256]).astype(BF)
        rest = lax.dynamic_index_in_dim(got[:, :, 256:288].reshape(2, 8, 16, 32), f, 1, keepdims=False)
        rhs2 = jnp.transpose(rest[:, :, :16], (1, 0, 2)).reshape(16, 32)
        rhs3 = jnp.transpose(rest[:, :, 16:], (1, 0, 2)).reshape(16, 32)
        y1 = mm(c1, a1).astype(BF)

    with jax.named_scope("level2_up"):
        half = lax.broadcasted_iota(jnp.int32, (16, 64), 1) // 32
        part = jnp.where(half == ib, jnp.concatenate([rhs2, rhs2], 1).astype(jnp.float32), 0.0) - mm(y1, g2)
        part = jnp.concatenate([part.astype(BF), jnp.pad(rhs3, ((0, 0), (0, 32)))], 1)
        got = lax.all_gather(part, "b")
        got, mixed, mixed_other, a3, a3_other, level3, level3_other = lax.optimization_barrier(
            (got, mixed, mixed_other, a3, a3_other, level3, level3_other)
        )
        mixed = ordered(mixed, mixed_other, ib, 0).reshape(512, 256)
        a2 = mixed[:, :64]
        h2 = mixed[:, 128:]
        a3 = ordered(a3, a3_other, ia, 0)
        a3_other = swap(a3, "b")
        level3 = ordered(level3, level3_other, ib, 1)
        level3_other = swap(level3, "c")
        c2 = total(got[:, :, :64]).astype(BF)
        rhs3 = jnp.transpose(got[:, :, 64:96], (1, 0, 2)).reshape(16, 64)
        got = spread(mm(c2, a2).astype(BF), "front")
        got, level3, level3_other = lax.optimization_barrier((got, level3, level3_other))
        level3 = ordered(level3, level3_other, ic, 2).reshape(128, 1536)
        g3 = level3[:, :512]
        b3 = level3[:, 512:]
        y2 = total(got).astype(BF)

    with jax.named_scope("level3_up"):
        half = lax.broadcasted_iota(jnp.int32, (16, 128), 1) // 64
        part = jnp.where(half == ia, jnp.concatenate([rhs3, rhs3], 1).astype(jnp.float32), 0.0) - mm(y2, g3)
        part = part.astype(BF)
        up = jnp.transpose(leaf_upper_inverse.reshape(128, 8, 128), (1, 0, 2))
        up, part = lax.optimization_barrier((up, part))
        up = exchange(up, "front")
        got = lax.all_gather(part, "a")
        got, up, a3, a3_other = lax.optimization_barrier((got, up, a3, a3_other))
        up = up.reshape(1024, 128)
        a3 = ordered(a3, a3_other, ib, 1).reshape(1024, 128)
        c3 = total(got).astype(BF)
        y3 = total(spread(mm(c3, a3).astype(BF), "front")).astype(BF)

    with jax.named_scope("level3_down"):
        z3 = mm(y3, b3).astype(BF)
        upper = lax.dot_general(hot, up, (((0,), (0,)), ((), ())), preferred_element_type=jnp.float32)
        upper = jnp.concatenate([upper.astype(BF), own_hot.T], 1)
        got = spread(mm(z3, h2).astype(BF), "front")
        got, upper = lax.optimization_barrier((got, upper))
        w2 = (y2.astype(jnp.float32) - total(got)).astype(BF)

    with jax.named_scope("local_down"):
        z2 = mm(w2, b2).astype(BF)
        w1 = (y1.astype(jnp.float32) - total(spread(mm(z2, h1).astype(BF), "front"))).astype(BF)
        z1 = mm(w1, b1).astype(BF)
        w_leaf = (y_leaf.astype(jnp.float32) - mm(z1, leaf_coupling_up)).astype(BF)
        own = jnp.concatenate(
            [
                w_leaf,
                columns(z1, ic * 8 + f, 16),
                columns(z2, 2 * ib + ic, 16),
                columns(z3, leaf, 16),
            ],
            1,
        )

    with jax.named_scope("leaf_upper"):
        out = mm(own, upper).astype(BF)
        out = jnp.transpose(out.reshape(16, 8, WIDE), (1, 0, 2))
        return total(exchange(out, "front"))[:, :176].astype(BF)


def solution(mesh):
    fronts = mesh.shape["front"]
    grid = Mesh(mesh.devices.reshape(-1, 2, 2, 2, fronts), AXES)
    rows = P(AXES, None)
    in_specs = (P(None, AXES), P(AXES[:4], None)) + (rows,) * 8
    return jax.shard_map(local, mesh=grid, in_specs=in_specs, out_specs=P(None, AXES), check_vma=False)
```

```python
import jax
import jax.numpy as jnp
from jax import lax
from jax.sharding import Mesh, PartitionSpec as P

AXES = ("sub", "a", "b", "c", "front")
PAIR = ("c", "front")
BF = jnp.bfloat16
WIDE = 256


def mm(x, w):
    return lax.dot_general(x, w, (((1,), (1,)), ((), ())), preferred_element_type=jnp.float32)


def exchange(x, axes):
    return lax.all_to_all(x, axes, 0, 0)


def copies(x, axes):
    return jnp.broadcast_to(x[None], (lax.axis_size(axes),) + x.shape)


def total(parts):
    return jnp.sum(parts.astype(jnp.float32), axis=0)


def swap(x, axis):
    return lax.ppermute(x, axis, [(0, 1), (1, 0)])


def ordered(mine, other, index, at):
    low = jnp.where(index == 0, mine, other)
    high = jnp.where(index == 0, other, mine)
    return jnp.stack([low, high], at)


def after(x, y):
    return lax.optimization_barrier((x, y))[0]


def tiles(m):
    return [m[:, i : i + 128] for i in range(0, m.shape[1], 128)]


def columns(m, index, width):
    return lax.dynamic_slice_in_dim(m, index * width, width, 1)


def local(
    basis,
    order,
    leaf_inverse,
    leaf_upper_inverse,
    leaf_coupling_low,
    leaf_coupling_up,
    sep_lower_inverse,
    sep_upper_inverse,
    sep_coupling_low,
    sep_coupling_up,
):
    ia, ib, ic = (lax.axis_index(n) for n in ("a", "b", "c"))
    f = lax.axis_index("front")
    leaf = 4 * ia + 2 * ib + ic

    with jax.named_scope("first_exchange"):

        def by_front(m, groups):
            m = jnp.transpose(m.reshape(-1, groups, 8, 16), (2, 0, 1, 3))
            return m.reshape(8, -1, groups * 16)

        def per_front(m):
            return jnp.broadcast_to(m[None], (2,) + m.shape).reshape((16,) + m.shape[1:])

        def for_all(m):
            return jnp.broadcast_to(m[None], (16,) + m.shape)

        low = jnp.transpose(leaf_coupling_low.reshape(16, 16, 128), (1, 0, 2))
        moved = jnp.concatenate(
            [
                for_all(jnp.pad(basis, ((0, 0), (0, 16)))),
                per_front(by_front(sep_lower_inverse[:, 256:768], 4)),
                for_all(sep_lower_inverse[:, :256]),
                low,
                per_front(by_front(sep_lower_inverse[:, 768:], 8)),
                per_front(by_front(sep_coupling_up[:, 512:], 8)),
            ],
            2,
        )
        got = exchange(moved, PAIR)

    with jax.named_scope("order"):
        place = (order[0] // 176) * WIDE + order[0] % 176
        slots = place.reshape(8, 176)
        leaf_place = slots[:, :128].reshape(1024)
        own_place = lax.dynamic_index_in_dim(slots, f, 0, keepdims=False)[128:]
        wide = 8 * WIDE
        hot = (leaf_place[:, None] == lax.broadcasted_iota(jnp.int32, (1024, wide), 1)).astype(BF)
        own_hot = (own_place[:, None] == lax.broadcasted_iota(jnp.int32, (48, wide), 1)).astype(BF)
        lower = lax.dot_general(leaf_inverse, hot, (((1,), (0,)), ((), ())), preferred_element_type=jnp.float32)
        lower = jnp.concatenate([lower.astype(BF), own_hot], 0)

    with jax.named_scope("planes_first"):
        g2 = sep_coupling_low[:, :512]
        more = jnp.concatenate([sep_upper_inverse[:, 256:768], sep_coupling_low[:, 512:]], 1)
        rows = jnp.concatenate([columns(g2, ib, 256), more], 1)
        rows_other = jnp.concatenate([columns(g2, 1 - ib, 256), more], 1)
        lower, rows_other = lax.optimization_barrier((lower, rows_other))
        rows_other = swap(rows_other, "b")

    got, rows, rows_other = lax.optimization_barrier((got, rows, rows_other))

    with jax.named_scope("unpack"):
        grouped = lax.dynamic_slice_in_dim(got[:, :, :WIDE], ic * 8, 8, 0)
        a2 = got[:, :, 192:256].reshape(256, 64)
        a1 = got[:, :, 256:512].reshape(256, 256)
        low_cols = got[:, :, 512:640].reshape(256, 128)
        a3 = got[:, :, 640:768].reshape(256, 128)
        h2 = got[:, :, 768:896].reshape(256, 128)
        rows = ordered(rows, rows_other, ib, 0).reshape(32, 1792)

    with jax.named_scope("planes_second"):
        level1 = jnp.concatenate([sep_upper_inverse[:, :256], sep_coupling_up[:, :512]], 1)
        level2 = jnp.concatenate([rows[:, :768], level1], 0)
        g3 = rows[:, 768:]
        tail = tiles(sep_upper_inverse[:, 768:]) + [a3]
        level3 = jnp.concatenate(tiles(columns(g3, ia, 512)) + tail, 0)
        level3_other = jnp.concatenate(tiles(columns(g3, 1 - ia, 512)) + tail, 0)
    with jax.named_scope("weights1"):
        row = lax.broadcasted_iota(jnp.int32, (384, 48), 0)
        col = lax.broadcasted_iota(jnp.int32, (384, 48), 1)
        target = jnp.where(col < 16, (ic * 8 + f) * 16 + col, 240 + col)
        keep = (row == target).astype(BF)
        first = jnp.concatenate([jnp.pad(-low_cols, ((0, 128), (0, 0))), keep], 1)

    with jax.named_scope("leaf_lower"):
        grouped = jnp.transpose(grouped, (1, 0, 2)).reshape(16, wide)
        own = mm(grouped, lower).astype(BF)
        y_leaf = own[:, :128]

    with jax.named_scope("level1_up"):
        sent = copies(mm(own, first).astype(BF), PAIR)
        level2_other = swap(after(level2, sent), "c")
        level3_other = swap(after(level3_other, sent), "a")
        got = exchange(sent, PAIR)
        got, level2, level2_other = lax.optimization_barrier((got, level2, level2_other))
        level2 = ordered(level2, level2_other, ic, 0)
        level1 = level2[:, 32:].reshape(32, 768)
        level2 = jnp.transpose(level2[:, :32].reshape(2, 2, 16, 768), (1, 0, 2, 3)).reshape(64, 768)
        g2 = level2[:, :256]
        b2 = level2[:, 256:]
        b1 = level1[:, :256]
        h1 = level1[:, 256:]
        c1 = total(got[:, :, :256]).astype(BF)
        rest = lax.dynamic_index_in_dim(got[:, :, 256:288].reshape(2, 8, 16, 32), f, 1, keepdims=False)
        rhs2 = jnp.transpose(rest[:, :, :16], (1, 0, 2)).reshape(16, 32)
        rhs3 = jnp.transpose(rest[:, :, 16:], (1, 0, 2)).reshape(16, 32)
        y1 = mm(c1, a1).astype(BF)

    with jax.named_scope("level2_up"):
        half = lax.broadcasted_iota(jnp.int32, (16, 64), 1) // 32
        part = jnp.where(half == ib, jnp.concatenate([rhs2, rhs2], 1).astype(jnp.float32), 0.0) - mm(y1, g2)
        part = jnp.concatenate([part.astype(BF), jnp.pad(rhs3, ((0, 0), (0, 32)))], 1)
        a2 = jnp.concatenate([a2[:128], a2[128:]], 1)
        got = lax.all_gather(jnp.concatenate([part, a2], 0), "b")
        a2 = jnp.concatenate([got[:, 16:144, :64], got[:, 16:144, 64:]], 1).reshape(512, 64)
        c2 = total(got[:, :16, :64]).astype(BF)
        rhs3 = jnp.transpose(got[:, :16, 64:96], (1, 0, 2)).reshape(16, 64)
        sent = copies(mm(c2, a2).astype(BF), "front")
        level3, level3_other = after((level3, level3_other), sent)
        level3 = ordered(level3, level3_other, ia, 0)
        g3 = level3[:, :128].reshape(256, 128)
        g3_other = swap(g3, "c")
        mixed = [level3[:, 256:].reshape(512, 128), level3[:, 128:256].reshape(256, 128), h2]
        mixed = jnp.concatenate(mixed, 0)
        mixed, g3_other = lax.optimization_barrier((mixed, g3_other))
        mixed_other = swap(mixed, "b")
        got = exchange(sent, "front")
        got, g3, g3_other = lax.optimization_barrier((got, g3, g3_other))
        g3 = ordered(g3, g3_other, ic, 0).reshape(2, 2, 4, 2, 16, 128)
        g3 = jnp.transpose(g3, (1, 3, 0, 4, 2, 5)).reshape(128, 512)
        y2 = total(got).astype(BF)

    with jax.named_scope("level3_up"):
        half = lax.broadcasted_iota(jnp.int32, (16, 128), 1) // 64
        part = jnp.where(half == ia, jnp.concatenate([rhs3, rhs3], 1).astype(jnp.float32), 0.0) - mm(y2, g3)
        part = part.astype(BF)
        up = jnp.transpose(leaf_upper_inverse.reshape(128, 8, 128), (1, 0, 2))
        down = by_front(h1, 4)
        down = jnp.concatenate([down[:, :16], down[:, 16:]], 2)
        whole = jnp.broadcast_to(jnp.concatenate(tiles(b1), 0)[None], (8, 64, 128))
        up = jnp.concatenate([up, whole, down], 1)
        up = after(up, y2)
        up = exchange(up, "front")
        got = lax.all_gather(part, "a")
        got, up, mixed, mixed_other = lax.optimization_barrier((got, up, mixed, mixed_other))
        b1 = jnp.transpose(up[:, 128:192].reshape(8, 2, 2, 16, 128), (2, 0, 3, 1, 4)).reshape(256, 256)
        h1 = jnp.transpose(up[:, 192:].reshape(8, 16, 2, 64), (2, 0, 1, 3)).reshape(256, 64)
        up = up[:, :128].reshape(1024, 128)
        mixed = ordered(mixed, mixed_other, ib, 0)
        a3 = jnp.transpose(mixed[:, :512].reshape(2, 2, 256, 128), (1, 0, 2, 3)).reshape(1024, 128)
        b3 = mixed[:, 512:768].reshape(512, 128)
        h2 = mixed[:, 768:].reshape(512, 128)
        c3 = total(got).astype(BF)
        sent = copies(mm(c3, a3).astype(BF), "front")
        b3_other = swap(after(b3, sent), "c")
        got = exchange(sent, "front")
        got, b3, b3_other = lax.optimization_barrier((got, b3, b3_other))
        b3 = ordered(b3, b3_other, ic, 0).reshape(2, 2, 2, 8, 16, 128)
        b3 = jnp.transpose(b3, (2, 1, 0, 4, 3, 5)).reshape(128, 1024)
        y3 = total(got).astype(BF)

    with jax.named_scope("level3_down"):
        z3 = mm(y3, b3).astype(BF)
        upper = lax.dot_general(hot, up, (((0,), (0,)), ((), ())), preferred_element_type=jnp.float32)
        upper = jnp.concatenate([upper.astype(BF), own_hot.T], 1)
        got = exchange(copies(mm(z3, h2).astype(BF), "front"), "front")
        got, upper = lax.optimization_barrier((got, upper))
        w2 = (y2.astype(jnp.float32) - total(got)).astype(BF)

    with jax.named_scope("local_down"):
        z2 = mm(w2, b2).astype(BF)
        w1 = (y1.astype(jnp.float32) - total(exchange(copies(mm(z2, h1).astype(BF), "front"), "front"))).astype(BF)
        z1 = mm(w1, b1).astype(BF)
        w_leaf = (y_leaf.astype(jnp.float32) - mm(z1, leaf_coupling_up)).astype(BF)
        own = jnp.concatenate(
            [
                w_leaf,
                columns(z1, ic * 8 + f, 16),
                columns(z2, 2 * ib + ic, 16),
                columns(z3, leaf, 16),
            ],
            1,
        )

    with jax.named_scope("leaf_upper"):
        out = mm(own, upper).astype(BF)
        out = jnp.transpose(out.reshape(16, 8, WIDE), (1, 0, 2))
        return total(exchange(out, "front"))[:, :176].astype(BF)


def solution(mesh):
    fronts = mesh.shape["front"]
    grid = Mesh(mesh.devices.reshape(-1, 2, 2, 2, fronts), AXES)
    rows = P(AXES, None)
    in_specs = (P(None, AXES), P(AXES[:4], None)) + (rows,) * 8
    return jax.shard_map(local, mesh=grid, in_specs=in_specs, out_specs=P(None, AXES), check_vma=False)
```

```python
import jax
import jax.numpy as jnp
from jax import lax
from jax.sharding import Mesh, PartitionSpec as P

AXES = ("sub", "a", "b", "c", "front")
PAIR = ("c", "front")
BF = jnp.bfloat16
WIDE = 256


def mm(x, w):
    return lax.dot_general(x, w, (((1,), (1,)), ((), ())), preferred_element_type=jnp.float32)


def exchange(x, axes):
    return lax.all_to_all(x, axes, 0, 0)


def copies(x, axes):
    return jnp.broadcast_to(x[None], (lax.axis_size(axes),) + x.shape)


def total(parts):
    return jnp.sum(parts.astype(jnp.float32), axis=0)


def swap(x, axis):
    return lax.ppermute(x, axis, [(0, 1), (1, 0)])


def ordered(mine, other, index, at):
    low = jnp.where(index == 0, mine, other)
    high = jnp.where(index == 0, other, mine)
    return jnp.stack([low, high], at)


def after(x, y):
    return lax.optimization_barrier((x, y))[0]


def tiles(m):
    return [m[:, i : i + 128] for i in range(0, m.shape[1], 128)]


def columns(m, index, width):
    return lax.dynamic_slice(m, (0, index * width), (m.shape[0], width), allow_negative_indices=False)


def window(m, start):
    return lax.dynamic_slice(m, (0, start), (m.shape[0], 16), allow_negative_indices=False)


def local(
    basis,
    order,
    leaf_inverse,
    leaf_upper_inverse,
    leaf_coupling_low,
    leaf_coupling_up,
    sep_lower_inverse,
    sep_upper_inverse,
    sep_coupling_low,
    sep_coupling_up,
):
    ia, ib, ic = (lax.axis_index(n) for n in ("a", "b", "c"))
    f = lax.axis_index("front")
    leaf = 4 * ia + 2 * ib + ic

    with jax.named_scope("first_exchange"):

        def by_front(m, groups):
            m = jnp.transpose(m.reshape(-1, groups, 8, 16), (2, 0, 1, 3))
            return m.reshape(8, -1, groups * 16)

        def per_front(m):
            return jnp.broadcast_to(m[None], (2,) + m.shape).reshape((16,) + m.shape[1:])

        def for_all(m):
            return jnp.broadcast_to(m[None], (16,) + m.shape)

        low = jnp.transpose(leaf_coupling_low.reshape(16, 16, 128), (1, 0, 2))
        moved = jnp.concatenate(
            [
                for_all(jnp.pad(basis, ((0, 0), (0, 16)))),
                per_front(by_front(sep_lower_inverse[:, 256:768], 4)),
                for_all(sep_lower_inverse[:, :256]),
                low,
                per_front(by_front(sep_lower_inverse[:, 768:], 8)),
                per_front(by_front(sep_coupling_up[:, 512:], 8)),
            ],
            2,
        )
        got = exchange(moved, PAIR)

    with jax.named_scope("order"):
        place = (order[0] // 176) * WIDE + order[0] % 176
        slots = place.reshape(8, 176)
        leaf_place = slots[:, :128].reshape(1024)
        own_place = lax.dynamic_index_in_dim(slots, f, 0, keepdims=False)[128:]
        wide = 8 * WIDE
        hot = (leaf_place[:, None] == lax.broadcasted_iota(jnp.int32, (1024, wide), 1)).astype(BF)
        own_hot = (own_place[:, None] == lax.broadcasted_iota(jnp.int32, (48, wide), 1)).astype(BF)
        lower = lax.dot_general(leaf_inverse, hot, (((1,), (0,)), ((), ())), preferred_element_type=jnp.float32)
        lower = jnp.concatenate([lower.astype(BF), own_hot], 0)

    with jax.named_scope("planes_first"):
        g2 = sep_coupling_low[:, :512]
        more = jnp.concatenate([sep_upper_inverse[:, 256:768], sep_coupling_low[:, 512:]], 1)
        rows = jnp.concatenate([columns(g2, ib, 256), more], 1)
        rows_other = jnp.concatenate([columns(g2, 1 - ib, 256), more], 1)
        lower, rows_other = lax.optimization_barrier((lower, rows_other))
        rows_other = swap(rows_other, "b")

    got, rows, rows_other = lax.optimization_barrier((got, rows, rows_other))

    with jax.named_scope("unpack"):
        grouped = lax.dynamic_slice_in_dim(got[:, :, :WIDE], ic * 8, 8, 0)
        a2 = got[:, :, 192:256].reshape(256, 64)
        a1 = got[:, :, 256:512].reshape(256, 256)
        low_cols = got[:, :, 512:640].reshape(256, 128)
        a3 = got[:, :, 640:768].reshape(256, 128)
        h2 = got[:, :, 768:896].reshape(256, 128)
        rows = ordered(rows, rows_other, ib, 0).reshape(32, 1792)

    with jax.named_scope("planes_second"):
        level1 = jnp.concatenate([sep_upper_inverse[:, :256], sep_coupling_up[:, :512]], 1)
        level2 = jnp.concatenate([rows[:, :768], level1], 0)
        g3 = rows[:, 768:]
        tail = tiles(sep_upper_inverse[:, 768:]) + [a3]
        level3 = jnp.concatenate(tiles(columns(g3, ia, 512)) + tail, 0)
        level3_other = jnp.concatenate(tiles(columns(g3, 1 - ia, 512)) + tail, 0)
    with jax.named_scope("weights1"):
        row = lax.broadcasted_iota(jnp.int32, (384, 48), 0)
        col = lax.broadcasted_iota(jnp.int32, (384, 48), 1)
        target = jnp.where(col < 16, (ic * 8 + f) * 16 + col, 240 + col)
        keep = (row == target).astype(BF)
        first = jnp.concatenate([jnp.pad(-low_cols, ((0, 128), (0, 0))), keep], 1)

    with jax.named_scope("leaf_lower"):
        grouped = jnp.transpose(grouped, (1, 0, 2)).reshape(16, wide)
        own = mm(grouped, lower).astype(BF)
        y_leaf = own[:, :128]

    with jax.named_scope("level1_up"):
        sent = copies(mm(own, first).astype(BF), PAIR)
        level2_other = swap(after(level2, sent), "c")
        level3_other = swap(after(level3_other, sent), "a")
        got = exchange(sent, PAIR)
        got, level2, level2_other = lax.optimization_barrier((got, level2, level2_other))
        level2 = ordered(level2, level2_other, ic, 0)
        level1 = level2[:, 32:].reshape(32, 768)
        level2 = jnp.transpose(level2[:, :32].reshape(2, 2, 16, 768), (1, 0, 2, 3)).reshape(64, 768)
        g2 = level2[:, :256]
        b2 = level2[:, 256:]
        b1 = level1[:, :256]
        h1 = level1[:, 256:]
        c1 = total(got[:, :, :256]).astype(BF)
        rest = lax.dynamic_index_in_dim(got[:, :, 256:288].reshape(2, 8, 16, 32), f, 1, keepdims=False)
        rhs2 = jnp.transpose(rest[:, :, :16], (1, 0, 2)).reshape(16, 32)
        rhs3 = jnp.transpose(rest[:, :, 16:], (1, 0, 2)).reshape(16, 32)
        y1 = mm(c1, a1).astype(BF)

    with jax.named_scope("level2_up"):
        half = lax.broadcasted_iota(jnp.int32, (16, 64), 1) // 32
        part = jnp.where(half == ib, jnp.concatenate([rhs2, rhs2], 1).astype(jnp.float32), 0.0) - mm(y1, g2)
        part = jnp.concatenate([part.astype(BF), jnp.pad(rhs3, ((0, 0), (0, 32)))], 1)
        a2 = jnp.concatenate([a2[:128], a2[128:]], 1)
        got = lax.all_gather(jnp.concatenate([part, a2], 0), "b")
        a2 = jnp.concatenate([got[:, 16:144, :64], got[:, 16:144, 64:]], 1).reshape(512, 64)
        c2 = total(got[:, :16, :64]).astype(BF)
        rhs3 = jnp.transpose(got[:, :16, 64:96], (1, 0, 2)).reshape(16, 64)
        up = jnp.transpose(leaf_upper_inverse.reshape(8, 16, 8, 128), (2, 1, 0, 3)).reshape(8, 16, 1024)
        whole = copies(jnp.concatenate([b1[:16], b1[16:]], 1), "front")
        down = by_front(h1, 4)
        extra = jnp.concatenate([up, whole, down[:, :16], down[:, 16:]], 2)
        sent = jnp.concatenate([copies(mm(c2, a2).astype(BF), "front"), extra], 2)
        level3, level3_other = after((level3, level3_other), sent)
        level3 = ordered(level3, level3_other, ia, 0)
        g3 = level3[:, :128].reshape(256, 128)
        g3 = lax.all_gather(g3, "c")
        mixed = [level3[:, 256:].reshape(512, 128), level3[:, 128:256].reshape(256, 128), h2]
        mixed = jnp.concatenate(mixed, 0)
        mixed, g3 = lax.optimization_barrier((mixed, g3))
        mixed_other = swap(mixed, "b")
        got = exchange(sent, "front")
        got, g3 = lax.optimization_barrier((got, g3))
        g3 = g3.reshape(2, 2, 4, 2, 16, 128)
        g3 = jnp.transpose(g3, (1, 3, 0, 4, 2, 5)).reshape(128, 512)
        y2 = total(got[:, :, :512]).astype(BF)
        extra = got[:, :, 512:]

    with jax.named_scope("level3_up"):
        half = lax.broadcasted_iota(jnp.int32, (16, 128), 1) // 64
        part = jnp.where(half == ia, jnp.concatenate([rhs3, rhs3], 1).astype(jnp.float32), 0.0) - mm(y2, g3)
        part = part.astype(BF)
        got = lax.all_gather(part, "a")
        got, mixed, mixed_other = lax.optimization_barrier((got, mixed, mixed_other))
        mixed = ordered(mixed, mixed_other, ib, 0)
        a3 = jnp.transpose(mixed[:, :512].reshape(2, 2, 256, 128), (1, 0, 2, 3)).reshape(1024, 128)
        b3 = mixed[:, 512:768].reshape(512, 128)
        h2 = mixed[:, 768:].reshape(512, 128)
        c3 = total(got).astype(BF)
        sent = copies(mm(c3, a3).astype(BF), "front")
        b3_other = swap(after(b3, sent), "c")
        got = exchange(sent, "front")
        extra = after(extra, sent)
        up = jnp.transpose(extra[:, :, :1024].reshape(8, 16, 8, 128), (0, 2, 1, 3)).reshape(1024, 128)
        b1 = jnp.transpose(extra[:, :, 1024:1536].reshape(8, 16, 2, 256), (2, 0, 1, 3)).reshape(256, 256)
        h1 = jnp.transpose(extra[:, :, 1536:].reshape(8, 16, 2, 64), (2, 0, 1, 3)).reshape(256, 64)
        upper = lax.dot_general(hot, up, (((0,), (0,)), ((), ())), preferred_element_type=jnp.float32)
        upper = jnp.concatenate([upper.astype(BF), own_hot.T], 1)
        got, b3, b3_other, upper, h1, b1, at1, at2, at3 = lax.optimization_barrier(
            (got, b3, b3_other, upper, h1, b1, (ic * 8 + f) * 16, (2 * ib + ic) * 16, leaf * 16)
        )
        b3 = ordered(b3, b3_other, ic, 0).reshape(2, 2, 2, 8, 16, 128)
        b3 = jnp.transpose(b3, (2, 1, 0, 4, 3, 5)).reshape(128, 1024)
        y3 = total(got).astype(BF)

    with jax.named_scope("level3_down"):
        z3 = mm(y3, b3).astype(BF)
        z3, own3 = lax.optimization_barrier((z3, window(z3, at3)))
        got = exchange(copies(mm(z3, h2).astype(BF), "front"), "front")
        w2 = (y2.astype(jnp.float32) - total(got)).astype(BF)

    with jax.named_scope("local_down"):
        z2 = mm(w2, b2).astype(BF)
        z2, own2 = lax.optimization_barrier((z2, window(z2, at2)))
        w1 = (y1.astype(jnp.float32) - total(exchange(copies(mm(z2, h1).astype(BF), "front"), "front"))).astype(BF)
        z1 = mm(w1, b1).astype(BF)
        w_leaf = (y_leaf.astype(jnp.float32) - mm(z1, leaf_coupling_up)).astype(BF)
        own = jnp.concatenate(
            [
                w_leaf,
                window(z1, at1),
                own2,
                own3,
            ],
            1,
        )

    with jax.named_scope("leaf_upper"):
        out = mm(own, upper).astype(BF)
        out = jnp.transpose(out.reshape(16, 8, WIDE), (1, 0, 2))
        return total(exchange(out, "front"))[:, :176].astype(BF)


def solution(mesh):
    fronts = mesh.shape["front"]
    grid = Mesh(mesh.devices.reshape(-1, 2, 2, 2, fronts), AXES)
    rows = P(AXES, None)
    in_specs = (P(None, AXES), P(AXES[:4], None)) + (rows,) * 8
    return jax.shard_map(local, mesh=grid, in_specs=in_specs, out_specs=P(None, AXES), check_vma=False)
```

```python
import jax
import jax.numpy as jnp
from jax import lax
from jax.experimental import pallas as pl
from jax.experimental.pallas import tpu as pltpu
from jax.sharding import Mesh, PartitionSpec as P

AXES = ("sub", "a", "b", "c", "front")
PAIR = ("c", "front")
BF = jnp.bfloat16
WIDE = 256


def mm(x, w):
    return lax.dot_general(x, w, (((1,), (1,)), ((), ())), preferred_element_type=jnp.float32)


def exchange(x, axes):
    return lax.all_to_all(x, axes, 0, 0)


def copies(x, axes):
    return jnp.broadcast_to(x[None], (lax.axis_size(axes),) + x.shape)


def total(parts):
    return jnp.sum(parts.astype(jnp.float32), axis=0)


def swap(x, axis):
    return lax.ppermute(x, axis, [(0, 1), (1, 0)])


def ordered(mine, other, index, at):
    low = jnp.where(index == 0, mine, other)
    high = jnp.where(index == 0, other, mine)
    return jnp.stack([low, high], at)


def after(x, y):
    return lax.optimization_barrier((x, y))[0]


def tiles(m):
    return [m[:, i : i + 128] for i in range(0, m.shape[1], 128)]


def columns(m, index, width):
    return lax.dynamic_slice(m, (0, index * width), (m.shape[0], width), allow_negative_indices=False)


def window(m, start):
    return lax.dynamic_slice(m, (0, start), (m.shape[0], 16), allow_negative_indices=False)


def pack_kernel(basis, lower, upper, low, out):
    group = lax.broadcasted_iota(jnp.int32, (16, 128), 1) // 16

    def pick(ref, at, count, front, first):
        chosen = jnp.zeros((16, 128), jnp.float32)
        for i in range(count):
            tile = ref[:, at + i * 128 : at + i * 128 + 128].astype(jnp.float32)
            shift = (first + i - front) % 8 * 16
            tile = pltpu.roll(tile, shift, 1) if shift else tile
            chosen = jnp.where(group == first + i, tile, chosen)
        return chosen

    base = jnp.concatenate([basis[:, 128:176].astype(jnp.float32), jnp.zeros((16, 80), jnp.float32)], 1)
    for front in range(8):
        mixed = jnp.where(group < 4, base, pick(lower, 256, 4, front, 4)).astype(BF)
        a3 = pick(lower, 768, 8, front, 0).astype(BF)
        h2 = pick(upper, 512, 8, front, 0).astype(BF)
        for peer in (front, front + 8):
            out[peer, :, 0:128] = basis[:, 0:128]
            out[peer, :, 128:256] = mixed
            out[peer, :, 256:512] = lower[:, 0:256]
            out[peer, :, 512:640] = low[:, peer * 128 : peer * 128 + 128]
            out[peer, :, 640:768] = a3
            out[peer, :, 768:896] = h2


def local(
    basis,
    order,
    leaf_inverse,
    leaf_upper_inverse,
    leaf_coupling_low,
    leaf_coupling_up,
    sep_lower_inverse,
    sep_upper_inverse,
    sep_coupling_low,
    sep_coupling_up,
):
    ia, ib, ic = (lax.axis_index(n) for n in ("a", "b", "c"))
    f = lax.axis_index("front")
    leaf = 4 * ia + 2 * ib + ic

    with jax.named_scope("first_exchange"):

        def by_front(m, groups):
            m = jnp.transpose(m.reshape(-1, groups, 8, 16), (2, 0, 1, 3))
            return m.reshape(8, -1, groups * 16)

        moved = pl.pallas_call(
            pack_kernel,
            out_shape=jax.ShapeDtypeStruct((16, 16, 896), BF),
            in_specs=[pl.BlockSpec(memory_space=pltpu.VMEM)] * 4,
            out_specs=pl.BlockSpec(memory_space=pltpu.VMEM),
        )(basis, sep_lower_inverse, sep_coupling_up, leaf_coupling_low)
        got = exchange(moved, PAIR)

    with jax.named_scope("order"):
        place = (order[0] // 176) * WIDE + order[0] % 176
        slots = place.reshape(8, 176)
        leaf_place = slots[:, :128].reshape(1024)
        own_place = lax.dynamic_index_in_dim(slots, f, 0, keepdims=False)[128:]
        wide = 8 * WIDE
        hot = (leaf_place[:, None] == lax.broadcasted_iota(jnp.int32, (1024, wide), 1)).astype(BF)
        own_hot = (own_place[:, None] == lax.broadcasted_iota(jnp.int32, (48, wide), 1)).astype(BF)
        lower = lax.dot_general(leaf_inverse, hot, (((1,), (0,)), ((), ())), preferred_element_type=jnp.float32)
        lower = jnp.concatenate([lower.astype(BF), own_hot], 0)

    with jax.named_scope("planes_first"):
        g2 = sep_coupling_low[:, :512]
        more = jnp.concatenate([sep_upper_inverse[:, 256:768], sep_coupling_low[:, 512:]], 1)
        rows = jnp.concatenate([columns(g2, ib, 256), more], 1)
        rows_other = jnp.concatenate([columns(g2, 1 - ib, 256), more], 1)
        level1 = jnp.concatenate([sep_upper_inverse[:, :256], sep_coupling_up[:, :512]], 1)
        b3 = jnp.concatenate(tiles(sep_upper_inverse[:, 768:]), 0)
        lower, rows_other, level1, b3 = lax.optimization_barrier((lower, rows_other, level1, b3))
        rows_other = swap(rows_other, "b")

    got, rows, rows_other = lax.optimization_barrier((got, rows, rows_other))

    with jax.named_scope("unpack"):
        grouped = lax.dynamic_slice_in_dim(got[:, :, :WIDE], ic * 8, 8, 0)
        a2 = got[:, :, 192:256].reshape(256, 64)
        a1 = got[:, :, 256:512].reshape(256, 256)
        low_cols = got[:, :, 512:640].reshape(256, 128)
        a3 = got[:, :, 640:768].reshape(256, 128)
        h2 = got[:, :, 768:896].reshape(256, 128)
        rows = ordered(rows, rows_other, ib, 0).reshape(32, 1792)

    with jax.named_scope("planes_second"):
        level2 = jnp.concatenate([rows[:, :768], level1], 0)
        g3 = rows[:, 768:]
        tail = [b3, a3]
        level3 = jnp.concatenate(tiles(columns(g3, ia, 512)) + tail, 0)
        level3_other = jnp.concatenate(tiles(columns(g3, 1 - ia, 512)) + tail, 0)
    with jax.named_scope("weights1"):
        row = lax.broadcasted_iota(jnp.int32, (384, 48), 0)
        col = lax.broadcasted_iota(jnp.int32, (384, 48), 1)
        target = jnp.where(col < 16, (ic * 8 + f) * 16 + col, 240 + col)
        keep = (row == target).astype(BF)
        first = jnp.concatenate([jnp.pad(-low_cols, ((0, 128), (0, 0))), keep], 1)

    with jax.named_scope("leaf_lower"):
        grouped = jnp.transpose(grouped, (1, 0, 2)).reshape(16, wide)
        own = mm(grouped, lower).astype(BF)
        y_leaf = own[:, :128]

    with jax.named_scope("level1_up"):
        sent = copies(mm(own, first).astype(BF), PAIR)
        level2_other = swap(after(level2, sent), "c")
        level3_other = swap(after(level3_other, sent), "a")
        got = exchange(sent, PAIR)
        got, level2, level2_other = lax.optimization_barrier((got, level2, level2_other))
        level2 = ordered(level2, level2_other, ic, 0)
        level1 = level2[:, 32:].reshape(32, 768)
        level2 = jnp.transpose(level2[:, :32].reshape(2, 2, 16, 768), (1, 0, 2, 3)).reshape(64, 768)
        g2 = level2[:, :256]
        b2 = level2[:, 256:]
        b1 = level1[:, :256]
        h1 = level1[:, 256:]
        c1 = total(got[:, :, :256]).astype(BF)
        rest = lax.dynamic_index_in_dim(got[:, :, 256:288].reshape(2, 8, 16, 32), f, 1, keepdims=False)
        rhs2 = jnp.transpose(rest[:, :, :16], (1, 0, 2)).reshape(16, 32)
        rhs3 = jnp.transpose(rest[:, :, 16:], (1, 0, 2)).reshape(16, 32)
        y1 = mm(c1, a1).astype(BF)

    with jax.named_scope("level2_up"):
        half = lax.broadcasted_iota(jnp.int32, (16, 64), 1) // 32
        part = jnp.where(half == ib, jnp.concatenate([rhs2, rhs2], 1).astype(jnp.float32), 0.0) - mm(y1, g2)
        part = jnp.concatenate([part.astype(BF), jnp.pad(rhs3, ((0, 0), (0, 32)))], 1)
        a2 = jnp.concatenate([a2[:128], a2[128:]], 1)
        got = lax.all_gather(jnp.concatenate([part, a2], 0), "b")
        a2 = jnp.concatenate([got[:, 16:144, :64], got[:, 16:144, 64:]], 1).reshape(512, 64)
        c2 = total(got[:, :16, :64]).astype(BF)
        rhs3 = jnp.transpose(got[:, :16, 64:96], (1, 0, 2)).reshape(16, 64)
        up = jnp.transpose(leaf_upper_inverse.reshape(8, 16, 8, 128), (2, 1, 0, 3)).reshape(8, 16, 1024)
        whole = copies(jnp.concatenate([b1[:16], b1[16:]], 1), "front")
        down = by_front(h1, 4)
        extra = jnp.concatenate([up, whole, down[:, :16], down[:, 16:]], 2)
        sent = jnp.concatenate([copies(mm(c2, a2).astype(BF), "front"), extra], 2)
        level3, level3_other = after((level3, level3_other), sent)
        level3 = ordered(level3, level3_other, ia, 0)
        g3 = level3[:, :128].reshape(256, 128)
        g3 = lax.all_gather(g3, "c")
        mixed = [level3[:, 256:].reshape(512, 128), level3[:, 128:256].reshape(256, 128), h2]
        mixed = jnp.concatenate(mixed, 0)
        mixed, g3 = lax.optimization_barrier((mixed, g3))
        mixed_other = swap(mixed, "b")
        got = exchange(sent, "front")
        got, g3 = lax.optimization_barrier((got, g3))
        g3 = g3.reshape(2, 2, 4, 2, 16, 128)
        g3 = jnp.transpose(g3, (1, 3, 0, 4, 2, 5)).reshape(128, 512)
        y2 = total(got[:, :, :512]).astype(BF)
        extra = got[:, :, 512:]

    with jax.named_scope("level3_up"):
        half = lax.broadcasted_iota(jnp.int32, (16, 128), 1) // 64
        part = jnp.where(half == ia, jnp.concatenate([rhs3, rhs3], 1).astype(jnp.float32), 0.0) - mm(y2, g3)
        part = part.astype(BF)
        got = lax.all_gather(part, "a")
        got, mixed, mixed_other = lax.optimization_barrier((got, mixed, mixed_other))
        mixed = ordered(mixed, mixed_other, ib, 0)
        a3 = jnp.transpose(mixed[:, :512].reshape(2, 2, 256, 128), (1, 0, 2, 3)).reshape(1024, 128)
        b3 = mixed[:, 512:768].reshape(512, 128)
        h2 = mixed[:, 768:].reshape(512, 128)
        c3 = total(got).astype(BF)
        sent = copies(mm(c3, a3).astype(BF), "front")
        b3_other = swap(after(b3, sent), "c")
        got = exchange(sent, "front")
        extra = after(extra, sent)
        up = jnp.transpose(extra[:, :, :1024].reshape(8, 16, 8, 128), (0, 2, 1, 3)).reshape(1024, 128)
        b1 = jnp.transpose(extra[:, :, 1024:1536].reshape(8, 16, 2, 256), (2, 0, 1, 3)).reshape(256, 256)
        h1 = jnp.transpose(extra[:, :, 1536:].reshape(8, 16, 2, 64), (2, 0, 1, 3)).reshape(256, 64)
        upper = lax.dot_general(hot, up, (((0,), (0,)), ((), ())), preferred_element_type=jnp.float32)
        upper = jnp.concatenate([upper.astype(BF), own_hot.T], 1)
        got, b3, b3_other, upper, h1, b1, at1, at2, at3 = lax.optimization_barrier(
            (got, b3, b3_other, upper, h1, b1, (ic * 8 + f) * 16, (2 * ib + ic) * 16, leaf * 16)
        )
        b3 = ordered(b3, b3_other, ic, 0).reshape(2, 2, 2, 8, 16, 128)
        b3 = jnp.transpose(b3, (2, 1, 0, 4, 3, 5)).reshape(128, 1024)
        y3 = total(got).astype(BF)

    with jax.named_scope("level3_down"):
        z3 = mm(y3, b3).astype(BF)
        z3, own3 = lax.optimization_barrier((z3, window(z3, at3)))
        got = exchange(copies(mm(z3, h2).astype(BF), "front"), "front")
        w2 = (y2.astype(jnp.float32) - total(got)).astype(BF)

    with jax.named_scope("local_down"):
        z2 = mm(w2, b2).astype(BF)
        z2, own2 = lax.optimization_barrier((z2, window(z2, at2)))
        w1 = (y1.astype(jnp.float32) - total(exchange(copies(mm(z2, h1).astype(BF), "front"), "front"))).astype(BF)
        z1 = mm(w1, b1).astype(BF)
        w_leaf = (y_leaf.astype(jnp.float32) - mm(z1, leaf_coupling_up)).astype(BF)
        own = jnp.concatenate(
            [
                w_leaf,
                window(z1, at1),
                own2,
                own3,
            ],
            1,
        )

    with jax.named_scope("leaf_upper"):
        out = mm(own, upper).astype(BF)
        out = jnp.transpose(out.reshape(16, 8, WIDE), (1, 0, 2))
        return total(exchange(out, "front"))[:, :176].astype(BF)


def solution(mesh):
    fronts = mesh.shape["front"]
    grid = Mesh(mesh.devices.reshape(-1, 2, 2, 2, fronts), AXES)
    rows = P(AXES, None)
    in_specs = (P(None, AXES), P(AXES[:4], None)) + (rows,) * 8
    return jax.shard_map(local, mesh=grid, in_specs=in_specs, out_specs=P(None, AXES), check_vma=False)
```

```python
import jax
import jax.numpy as jnp
from jax import lax
from jax.experimental import pallas as pl
from jax.experimental.pallas import tpu as pltpu
from jax.sharding import Mesh, PartitionSpec as P

AXES = ("sub", "a", "b", "c", "front")
PAIR = ("c", "front")
BF = jnp.bfloat16
WIDE = 256


def mm(x, w):
    return lax.dot_general(x, w, (((1,), (1,)), ((), ())), preferred_element_type=jnp.float32)


def exchange(x, axes):
    return lax.all_to_all(x, axes, 0, 0)


def copies(x, axes):
    return jnp.broadcast_to(x[None], (lax.axis_size(axes),) + x.shape)


def total(parts):
    return jnp.sum(parts.astype(jnp.float32), axis=0)


def swap(x, axis):
    return lax.ppermute(x, axis, [(0, 1), (1, 0)])


def ordered(mine, other, index, at):
    low = jnp.where(index == 0, mine, other)
    high = jnp.where(index == 0, other, mine)
    return jnp.stack([low, high], at)


def after(x, y):
    return lax.optimization_barrier((x, y))[0]


def tiles(m):
    return [m[:, i : i + 128] for i in range(0, m.shape[1], 128)]


def columns(m, index, width):
    return lax.dynamic_slice(m, (0, index * width), (m.shape[0], width), allow_negative_indices=False)


def window(m, start):
    return lax.dynamic_slice(m, (0, start), (m.shape[0], 16), allow_negative_indices=False)


def pack_kernel(basis, lower, upper, low, out):
    group = lax.broadcasted_iota(jnp.int32, (16, 128), 1) // 16

    def pick(ref, at, count, front, first, step=128):
        chosen = jnp.zeros((16, 128), jnp.float32)
        for i in range(count):
            tile = ref[:, at + i * step : at + i * step + 128].astype(jnp.float32)
            shift = (first + i - front) % 8 * 16
            tile = pltpu.roll(tile, shift, 1) if shift else tile
            chosen = jnp.where(group == first + i, tile, chosen)
        return chosen

    base = jnp.concatenate([basis[:, 128:176].astype(jnp.float32), jnp.zeros((16, 80), jnp.float32)], 1)
    for front in range(8):
        mixed = jnp.where(group < 4, base, pick(lower, 256, 4, front, 4)).astype(BF)
        a3 = pick(lower, 768, 8, front, 0).astype(BF)
        for peer in (front, front + 8):
            h2 = pick(upper, 512 + peer // 8 * 128, 4, front, 0, 256).astype(BF)
            out[peer, :, 0:128] = basis[:, 0:128]
            out[peer, :, 128:256] = mixed
            out[peer, :, 256:512] = lower[:, 0:256]
            out[peer, :, 512:640] = low[:, peer * 128 : peer * 128 + 128]
            out[peer, :, 640:768] = a3
            out[peer, :, 768:896] = h2


def local(
    basis,
    order,
    leaf_inverse,
    leaf_upper_inverse,
    leaf_coupling_low,
    leaf_coupling_up,
    sep_lower_inverse,
    sep_upper_inverse,
    sep_coupling_low,
    sep_coupling_up,
):
    ia, ib, ic = (lax.axis_index(n) for n in ("a", "b", "c"))
    f = lax.axis_index("front")

    with jax.named_scope("first_exchange"):

        def by_front(m, groups):
            m = jnp.transpose(m.reshape(-1, groups, 8, 16), (2, 0, 1, 3))
            return m.reshape(8, -1, groups * 16)

        moved = pl.pallas_call(
            pack_kernel,
            out_shape=jax.ShapeDtypeStruct((16, 16, 896), BF),
            in_specs=[pl.BlockSpec(memory_space=pltpu.VMEM)] * 4,
            out_specs=pl.BlockSpec(memory_space=pltpu.VMEM),
        )(basis, sep_lower_inverse, sep_coupling_up, leaf_coupling_low)
        got = exchange(moved, PAIR)

    with jax.named_scope("order"):
        place = (order[0] // 176) * WIDE + order[0] % 176
        slots = place.reshape(8, 176)
        leaf_place = slots[:, :128].reshape(1024)
        own_place = lax.dynamic_index_in_dim(slots, f, 0, keepdims=False)[128:]
        wide = 8 * WIDE
        hot = (leaf_place[:, None] == lax.broadcasted_iota(jnp.int32, (1024, wide), 1)).astype(BF)
        own_hot = (own_place[:, None] == lax.broadcasted_iota(jnp.int32, (48, wide), 1)).astype(BF)
        lower = lax.dot_general(leaf_inverse, hot, (((1,), (0,)), ((), ())), preferred_element_type=jnp.float32)
        lower = jnp.concatenate([lower.astype(BF), own_hot], 0)

    with jax.named_scope("planes_first"):
        g2 = sep_coupling_low[:, :512]
        g3 = sep_coupling_low[:, 512:]
        rows = jnp.concatenate([columns(g2, ib, 256), g3], 1)
        rows_other = jnp.concatenate([columns(g2, 1 - ib, 256), g3], 1)
        level1 = jnp.concatenate([sep_upper_inverse[:, :256], sep_coupling_up[:, :512]], 1)
        b3 = jnp.concatenate(tiles(sep_upper_inverse[:, 768:]), 0)
        b2 = jnp.concatenate(tiles(sep_upper_inverse[:, 256:768]), 0)
        lower, rows_other, level1, b3, b2 = lax.optimization_barrier((lower, rows_other, level1, b3, b2))
        rows_other = swap(rows_other, "b")

    got, rows, rows_other = lax.optimization_barrier((got, rows, rows_other))

    with jax.named_scope("unpack"):
        grouped = lax.dynamic_slice_in_dim(got[:, :, :WIDE], ic * 8, 8, 0)
        a2 = got[:, :, 192:256].reshape(256, 64)
        a1 = got[:, :, 256:512].reshape(256, 256)
        low_cols = got[:, :, 512:640].reshape(256, 128)
        a3 = got[:, :, 640:768].reshape(256, 128)
        h2 = got[:, :, 768:832].reshape(256, 64)
        rows = ordered(rows, rows_other, ib, 0).reshape(32, 1280)

    with jax.named_scope("planes_second"):
        g2 = jnp.concatenate([rows[:16, :256], rows[16:, :256], rows[:16, :256]], 1)
        level2 = jnp.concatenate([g2, level1], 0)
        g3 = rows[:, 256:]
        tail = [b3, a3]
        level3 = jnp.concatenate(tiles(columns(g3, ia, 512)) + tail, 0)
        level3_other = jnp.concatenate(tiles(columns(g3, 1 - ia, 512)) + tail, 0)
    with jax.named_scope("weights1"):
        row = lax.broadcasted_iota(jnp.int32, (384, 48), 0)
        col = lax.broadcasted_iota(jnp.int32, (384, 48), 1)
        target = jnp.where(col < 16, (ic * 8 + f) * 16 + col, 240 + col)
        keep = (row == target).astype(BF)
        first = jnp.concatenate([jnp.pad(-low_cols, ((0, 128), (0, 0))), keep], 1)

    with jax.named_scope("leaf_lower"):
        grouped = jnp.transpose(grouped, (1, 0, 2)).reshape(16, wide)
        own = mm(grouped, lower).astype(BF)
        y_leaf = own[:, :128]

    with jax.named_scope("level1_up"):
        sent = copies(mm(own, first).astype(BF), PAIR)
        level2_other = swap(after(level2, sent), "c")
        level3_other = swap(after(level3_other, sent), "a")
        got = exchange(sent, PAIR)
        got, level2, level2_other = lax.optimization_barrier((got, level2, level2_other))
        level2 = ordered(level2, level2_other, ic, 0)
        level1 = level2[:, 16:].reshape(32, 768)
        g2 = jnp.stack([level2[:, :16, :256], level2[:, :16, 256:512]], 0).reshape(64, 256)
        b1 = level1[:, :256]
        h1 = level1[:, 256:]
        c1 = total(got[:, :, :256]).astype(BF)
        rest = lax.dynamic_index_in_dim(got[:, :, 256:288].reshape(2, 8, 16, 32), f, 1, keepdims=False)
        rhs2 = jnp.transpose(rest[:, :, :16], (1, 0, 2)).reshape(16, 32)
        rhs3 = jnp.transpose(rest[:, :, 16:], (1, 0, 2)).reshape(16, 32)
        y1 = mm(c1, a1).astype(BF)

    with jax.named_scope("level2_up"):
        half = lax.broadcasted_iota(jnp.int32, (16, 64), 1) // 32
        part = jnp.where(half == ib, jnp.concatenate([rhs2, rhs2], 1).astype(jnp.float32), 0.0) - mm(y1, g2)
        part = jnp.concatenate([part.astype(BF), jnp.pad(rhs3, ((0, 0), (0, 32)))], 1)
        a2 = jnp.concatenate([a2[:128], a2[128:]], 1)
        got = lax.all_gather(jnp.concatenate([part, a2], 0), "b")
        a2 = jnp.concatenate([got[:, 16:144, :64], got[:, 16:144, 64:]], 1).reshape(512, 64)
        c2 = total(got[:, :16, :64]).astype(BF)
        rhs3 = jnp.transpose(got[:, :16, 64:96], (1, 0, 2)).reshape(16, 64)
        up = jnp.transpose(leaf_upper_inverse.reshape(8, 16, 8, 128), (2, 1, 0, 3)).reshape(8, 16, 1024)
        whole = copies(jnp.concatenate([b1[:16], b1[16:]], 1), "front")
        down = by_front(h1, 4)
        extra = jnp.concatenate([up, whole, down[:, :16], down[:, 16:]], 2)
        sent = jnp.concatenate([copies(mm(c2, a2).astype(BF), "front"), extra], 2)
        level3, level3_other = after((level3, level3_other), sent)
        level3 = ordered(level3, level3_other, ia, 0)
        g3 = jnp.concatenate([level3[:, :128].reshape(256, 128), b2], 0)
        g3 = lax.all_gather(g3, "c")
        b2 = g3[:, 256:].reshape(128, 128)
        g3 = g3[:, :256]
        mixed = [level3[:, 256:].reshape(512, 128), level3[:, 128:256].reshape(256, 128)]
        mixed = jnp.concatenate(mixed + [jnp.concatenate([h2[:128], h2[128:]], 1), b2], 0)
        mixed, g3 = lax.optimization_barrier((mixed, g3))
        mixed_other = swap(mixed, "b")
        got = exchange(sent, "front")
        got, g3 = lax.optimization_barrier((got, g3))
        g3 = g3.reshape(2, 2, 4, 2, 16, 128)
        g3 = jnp.transpose(g3, (1, 3, 0, 4, 2, 5)).reshape(128, 512)
        y2 = total(got[:, :, :512]).astype(BF)
        extra = got[:, :, 512:]

    with jax.named_scope("level3_up"):
        half = lax.broadcasted_iota(jnp.int32, (16, 128), 1) // 64
        part = jnp.where(half == ia, jnp.concatenate([rhs3, rhs3], 1).astype(jnp.float32), 0.0) - mm(y2, g3)
        part = part.astype(BF)
        got = lax.all_gather(part, "a")
        up = jnp.transpose(extra[:, :, :1024].reshape(8, 16, 8, 128), (0, 2, 1, 3)).reshape(1024, 128)
        b1 = jnp.transpose(extra[:, :, 1024:1536].reshape(8, 16, 2, 256), (2, 0, 1, 3)).reshape(256, 256)
        h1 = jnp.transpose(extra[:, :, 1536:].reshape(8, 16, 2, 64), (2, 0, 1, 3)).reshape(256, 64)
        upper = lax.dot_general(hot, up, (((0,), (0,)), ((), ())), preferred_element_type=jnp.float32)
        upper = jnp.concatenate([upper.astype(BF), own_hot.T], 1)
        at1, at2, at3 = (ic * 8 + f) * 16, (2 * ib + ic) * 16, (2 * ia + ib) * 16
        got, mixed, mixed_other, upper, h1, b1, at1, at2, at3 = lax.optimization_barrier(
            (got, mixed, mixed_other, upper, h1, b1, at1, at2, at3)
        )
        mixed = ordered(mixed, mixed_other, ib, 0)
        a3 = jnp.transpose(mixed[:, :512].reshape(2, 2, 256, 128), (1, 0, 2, 3)).reshape(1024, 128)
        b3 = mixed[:, 512:768].reshape(2, 2, 8, 16, 128)
        b3 = jnp.transpose(b3, (1, 0, 3, 2, 4)).reshape(64, 1024)
        h2 = jnp.concatenate([mixed[:, 768:896, :64], mixed[:, 768:896, 64:]], 1).reshape(512, 64)
        b2 = jnp.transpose(mixed[:, 896:].reshape(2, 2, 4, 16, 128), (0, 1, 3, 2, 4)).reshape(64, 512)
        got, b3, b2, h2 = lax.optimization_barrier((got, b3, b2, h2))
        c3 = total(got).astype(BF)
        sent = copies(mm(c3, a3).astype(BF), "front")
        got = exchange(sent, "front")
        y3 = total(got).astype(BF)

    with jax.named_scope("level3_down"):
        z3 = mm(y3, b3).astype(BF)
        z3, own3 = lax.optimization_barrier((z3, window(z3, at3)))
        got = exchange(copies(mm(z3, h2).astype(BF), PAIR), PAIR)
        w2 = (y2.astype(jnp.float32) - total(got)).astype(BF)

    with jax.named_scope("local_down"):
        z2 = mm(w2, b2).astype(BF)
        z2, own2 = lax.optimization_barrier((z2, window(z2, at2)))
        w1 = (y1.astype(jnp.float32) - total(exchange(copies(mm(z2, h1).astype(BF), "front"), "front"))).astype(BF)
        z1 = mm(w1, b1).astype(BF)
        w_leaf = (y_leaf.astype(jnp.float32) - mm(z1, leaf_coupling_up)).astype(BF)
        own = jnp.concatenate(
            [
                w_leaf,
                window(z1, at1),
                own2,
                own3,
            ],
            1,
        )

    with jax.named_scope("leaf_upper"):
        out = mm(own, upper).astype(BF)
        out = jnp.transpose(out.reshape(16, 8, WIDE), (1, 0, 2))
        return total(exchange(out, "front"))[:, :176].astype(BF)


def solution(mesh):
    fronts = mesh.shape["front"]
    grid = Mesh(mesh.devices.reshape(-1, 2, 2, 2, fronts), AXES)
    rows = P(AXES, None)
    in_specs = (P(None, AXES), P(AXES[:4], None)) + (rows,) * 8
    return jax.shard_map(local, mesh=grid, in_specs=in_specs, out_specs=P(None, AXES), check_vma=False)
```

```python
import jax
import jax.numpy as jnp
from jax import lax
from jax.experimental import pallas as pl
from jax.experimental.pallas import tpu as pltpu
from jax.sharding import Mesh, PartitionSpec as P

AXES = ("sub", "a", "b", "c", "front")
PAIR = ("c", "front")
BF = jnp.bfloat16
WIDE = 256


def mm(x, w):
    return lax.dot_general(x, w, (((1,), (1,)), ((), ())), preferred_element_type=jnp.float32)


def exchange(x, axes):
    return lax.all_to_all(x, axes, 0, 0)


def copies(x, axes):
    return jnp.broadcast_to(x[None], (lax.axis_size(axes),) + x.shape)


def total(parts):
    return jnp.sum(parts.astype(jnp.float32), axis=0)


def swap(x, axis):
    return lax.ppermute(x, axis, [(0, 1), (1, 0)])


def ordered(mine, other, index, at):
    low = jnp.where(index == 0, mine, other)
    high = jnp.where(index == 0, other, mine)
    return jnp.stack([low, high], at)


def after(x, y):
    return lax.optimization_barrier((x, y))[0]


def tiles(m):
    return [m[:, i : i + 128] for i in range(0, m.shape[1], 128)]


def columns(m, index, width):
    return lax.dynamic_slice(m, (0, index * width), (m.shape[0], width), allow_negative_indices=False)


def window(m, start):
    return lax.dynamic_slice(m, (0, start), (m.shape[0], 16), allow_negative_indices=False)


def pack_kernel(basis, lower, upper, low, out):
    group = lax.broadcasted_iota(jnp.int32, (16, 128), 1) // 16

    def pick(ref, at, count, front, first, step=128):
        chosen = jnp.zeros((16, 128), jnp.float32)
        for i in range(count):
            tile = ref[:, at + i * step : at + i * step + 128].astype(jnp.float32)
            shift = (first + i - front) % 8 * 16
            tile = pltpu.roll(tile, shift, 1) if shift else tile
            chosen = jnp.where(group == first + i, tile, chosen)
        return chosen

    base = jnp.concatenate([basis[:, 128:176].astype(jnp.float32), jnp.zeros((16, 80), jnp.float32)], 1)
    for front in range(8):
        mixed = jnp.where(group < 4, base, pick(lower, 256, 4, front, 4)).astype(BF)
        a3 = pick(lower, 768, 8, front, 0).astype(BF)
        for peer in (front, front + 8):
            h2 = pick(upper, 512 + peer // 8 * 128, 4, front, 0, 256).astype(BF)
            out[peer, :, 0:128] = basis[:, 0:128]
            out[peer, :, 128:256] = mixed
            out[peer, :, 256:512] = lower[:, 0:256]
            out[peer, :, 512:640] = low[:, peer * 128 : peer * 128 + 128]
            out[peer, :, 640:768] = a3
            out[peer, :, 768:896] = h2


def local(
    basis,
    order,
    leaf_inverse,
    leaf_upper_inverse,
    leaf_coupling_low,
    leaf_coupling_up,
    sep_lower_inverse,
    sep_upper_inverse,
    sep_coupling_low,
    sep_coupling_up,
):
    ia, ib, ic = (lax.axis_index(n) for n in ("a", "b", "c"))
    f = lax.axis_index("front")

    with jax.named_scope("first_exchange"):

        def by_front(m, groups):
            m = jnp.transpose(m.reshape(-1, groups, 8, 16), (2, 0, 1, 3))
            return m.reshape(8, -1, groups * 16)

        moved = pl.pallas_call(
            pack_kernel,
            out_shape=jax.ShapeDtypeStruct((16, 16, 896), BF),
            in_specs=[pl.BlockSpec(memory_space=pltpu.VMEM)] * 4,
            out_specs=pl.BlockSpec(memory_space=pltpu.VMEM),
        )(basis, sep_lower_inverse, sep_coupling_up, leaf_coupling_low)
        got = exchange(moved, PAIR)

    with jax.named_scope("order"):
        place = (order[0] // 176) * WIDE + order[0] % 176
        slots = place.reshape(8, 176)
        leaf_place = slots[:, :128].reshape(1024)
        own_place = lax.dynamic_index_in_dim(slots, f, 0, keepdims=False)[128:]
        wide = 8 * WIDE
        leaf_place = leaf_place.astype(jnp.int16)
        hot = (leaf_place[:, None] == lax.broadcasted_iota(jnp.int16, (1024, wide), 1)).astype(BF)
        own_hot = (own_place[:, None] == lax.broadcasted_iota(jnp.int32, (48, wide), 1)).astype(BF)
        lower = lax.dot_general(leaf_inverse, hot, (((1,), (0,)), ((), ())), preferred_element_type=jnp.float32)
        lower = jnp.concatenate([lower.astype(BF), own_hot], 0)

    with jax.named_scope("planes_first"):
        g2 = sep_coupling_low[:, :512]
        g3 = sep_coupling_low[:, 512:]
        rows = jnp.concatenate([columns(g2, ib, 256), g3], 1)
        rows_other = jnp.concatenate([columns(g2, 1 - ib, 256), g3], 1)
        level1 = jnp.concatenate([sep_upper_inverse[:, :256], sep_coupling_up[:, :512]], 1)
        b3 = jnp.concatenate(tiles(sep_upper_inverse[:, 768:]), 0)
        b2 = jnp.concatenate(tiles(sep_upper_inverse[:, 256:768]), 0)
        lower, rows_other, level1, b3, b2 = lax.optimization_barrier((lower, rows_other, level1, b3, b2))
        rows_other = swap(rows_other, "b")

    got, rows, rows_other = lax.optimization_barrier((got, rows, rows_other))

    with jax.named_scope("unpack"):
        grouped = lax.dynamic_slice_in_dim(got[:, :, :WIDE], ic * 8, 8, 0)
        a2 = got[:, :, 192:256].reshape(256, 64)
        a1 = got[:, :, 256:512].reshape(256, 256)
        low_cols = got[:, :, 512:640].reshape(256, 128)
        a3 = got[:, :, 640:768].reshape(256, 128)
        h2 = got[:, :, 768:832].reshape(256, 64)
        rows = ordered(rows, rows_other, ib, 0).reshape(32, 1280)

    with jax.named_scope("planes_second"):
        g2 = jnp.concatenate([rows[:16, :256], rows[16:, :256], rows[:16, :256]], 1)
        level2 = jnp.concatenate([g2, level1], 0)
        g3 = rows[:, 256:]
        tail = [b3, a3]
        level3 = jnp.concatenate(tiles(columns(g3, ia, 512)) + tail, 0)
        level3_other = jnp.concatenate(tiles(columns(g3, 1 - ia, 512)) + tail, 0)
    with jax.named_scope("weights1"):
        row = lax.broadcasted_iota(jnp.int32, (384, 48), 0)
        col = lax.broadcasted_iota(jnp.int32, (384, 48), 1)
        target = jnp.where(col < 16, (ic * 8 + f) * 16 + col, 240 + col)
        keep = (row == target).astype(BF)
        first = jnp.concatenate([jnp.pad(-low_cols, ((0, 128), (0, 0))), keep], 1)

    with jax.named_scope("leaf_lower"):
        grouped = jnp.transpose(grouped, (1, 0, 2)).reshape(16, wide)
        own = mm(grouped, lower).astype(BF)
        y_leaf = own[:, :128]

    with jax.named_scope("level1_up"):
        sent = copies(mm(own, first).astype(BF), PAIR)
        level2_other = swap(after(level2, sent), "c")
        level3_other = swap(after(level3_other, sent), "a")
        got = exchange(sent, PAIR)
        got, level2, level2_other = lax.optimization_barrier((got, level2, level2_other))
        level2 = ordered(level2, level2_other, ic, 0)
        level1 = level2[:, 16:].reshape(32, 768)
        g2 = jnp.stack([level2[:, :16, :256], level2[:, :16, 256:512]], 0).reshape(64, 256)
        b1 = level1[:, :256]
        h1 = level1[:, 256:]
        c1 = total(got[:, :, :256]).astype(BF)
        rest = lax.dynamic_index_in_dim(got[:, :, 256:288].reshape(2, 8, 16, 32), f, 1, keepdims=False)
        rhs2 = jnp.transpose(rest[:, :, :16], (1, 0, 2)).reshape(16, 32)
        rhs3 = jnp.transpose(rest[:, :, 16:], (1, 0, 2)).reshape(16, 32)
        y1 = mm(c1, a1).astype(BF)

    with jax.named_scope("level2_up"):
        half = lax.broadcasted_iota(jnp.int32, (16, 64), 1) // 32
        part = jnp.where(half == ib, jnp.concatenate([rhs2, rhs2], 1).astype(jnp.float32), 0.0) - mm(y1, g2)
        part = jnp.concatenate([part.astype(BF), jnp.pad(rhs3, ((0, 0), (0, 32)))], 1)
        a2 = jnp.concatenate([a2[:128], a2[128:]], 1)
        got = lax.all_gather(jnp.concatenate([part, a2], 0), "b")
        a2 = jnp.concatenate([got[:, 16:144, :64], got[:, 16:144, 64:]], 1).reshape(512, 64)
        c2 = total(got[:, :16, :64]).astype(BF)
        rhs3 = jnp.transpose(got[:, :16, 64:96], (1, 0, 2)).reshape(16, 64)
        up = jnp.transpose(leaf_upper_inverse.reshape(8, 16, 8, 128), (2, 1, 0, 3)).reshape(8, 16, 1024)
        whole = copies(jnp.concatenate([b1[:16], b1[16:]], 1), "front")
        down = by_front(h1, 4)
        extra = jnp.concatenate([up, whole, down[:, :16], down[:, 16:]], 2)
        sent = jnp.concatenate([copies(mm(c2, a2).astype(BF), "front"), extra], 2)
        level3, level3_other = after((level3, level3_other), sent)
        level3 = ordered(level3, level3_other, ia, 0)
        g3 = jnp.concatenate([level3[:, :128].reshape(256, 128), b2], 0)
        g3 = lax.all_gather(g3, "c")
        b2 = g3[:, 256:].reshape(128, 128)
        g3 = g3[:, :256]
        mixed = [level3[:, 256:].reshape(512, 128), level3[:, 128:256].reshape(256, 128)]
        mixed = jnp.concatenate(mixed + [jnp.concatenate([h2[:128], h2[128:]], 1), b2], 0)
        mixed, g3 = lax.optimization_barrier((mixed, g3))
        mixed_other = swap(mixed, "b")
        got = exchange(sent, "front")
        got, g3 = lax.optimization_barrier((got, g3))
        g3 = g3.reshape(2, 2, 4, 2, 16, 128)
        g3 = jnp.transpose(g3, (1, 3, 0, 4, 2, 5)).reshape(128, 512)
        y2 = total(got[:, :, :512]).astype(BF)
        extra = got[:, :, 512:]

    with jax.named_scope("level3_up"):
        half = lax.broadcasted_iota(jnp.int32, (16, 128), 1) // 64
        part = jnp.where(half == ia, jnp.concatenate([rhs3, rhs3], 1).astype(jnp.float32), 0.0) - mm(y2, g3)
        part = part.astype(BF)
        got = lax.all_gather(part, "a")
        up = jnp.transpose(extra[:, :, :1024].reshape(8, 16, 8, 128), (0, 2, 1, 3)).reshape(1024, 128)
        b1 = jnp.transpose(extra[:, :, 1024:1536].reshape(8, 16, 2, 256), (2, 0, 1, 3)).reshape(256, 256)
        h1 = jnp.transpose(extra[:, :, 1536:].reshape(8, 16, 2, 64), (2, 0, 1, 3)).reshape(256, 64)
        upper = lax.dot_general(hot, up, (((0,), (0,)), ((), ())), preferred_element_type=jnp.float32)
        upper = jnp.concatenate([upper.astype(BF), own_hot.T], 1)
        at1, at2, at3 = (ic * 8 + f) * 16, (2 * ib + ic) * 16, (2 * ia + ib) * 16
        got, mixed, mixed_other, upper, h1, b1, at1, at2, at3 = lax.optimization_barrier(
            (got, mixed, mixed_other, upper, h1, b1, at1, at2, at3)
        )
        mixed = ordered(mixed, mixed_other, ib, 0)
        a3 = jnp.transpose(mixed[:, :512].reshape(2, 2, 256, 128), (1, 0, 2, 3)).reshape(1024, 128)
        b3 = mixed[:, 512:768].reshape(2, 2, 8, 16, 128)
        b3 = jnp.transpose(b3, (1, 0, 3, 2, 4)).reshape(64, 1024)
        h2 = jnp.concatenate([mixed[:, 768:896, :64], mixed[:, 768:896, 64:]], 1).reshape(512, 64)
        b2 = jnp.transpose(mixed[:, 896:].reshape(2, 2, 4, 16, 128), (0, 1, 3, 2, 4)).reshape(64, 512)
        got, b3, b2, h2 = lax.optimization_barrier((got, b3, b2, h2))
        c3 = total(got).astype(BF)
        sent = copies(mm(c3, a3).astype(BF), "front")
        got = exchange(sent, "front")
        y3 = total(got).astype(BF)

    with jax.named_scope("level3_down"):
        z3 = mm(y3, b3).astype(BF)
        z3, own3 = lax.optimization_barrier((z3, window(z3, at3)))
        got = exchange(copies(mm(z3, h2).astype(BF), PAIR), PAIR)
        w2 = (y2.astype(jnp.float32) - total(got)).astype(BF)

    with jax.named_scope("local_down"):
        z2 = mm(w2, b2).astype(BF)
        z2, own2 = lax.optimization_barrier((z2, window(z2, at2)))
        w1 = (y1.astype(jnp.float32) - total(exchange(copies(mm(z2, h1).astype(BF), "front"), "front"))).astype(BF)
        z1 = mm(w1, b1).astype(BF)
        w_leaf = (y_leaf.astype(jnp.float32) - mm(z1, leaf_coupling_up)).astype(BF)
        own = jnp.concatenate(
            [
                w_leaf,
                window(z1, at1),
                own2,
                own3,
            ],
            1,
        )

    with jax.named_scope("leaf_upper"):
        out = mm(own, upper).astype(BF)
        out = jnp.transpose(out.reshape(16, 8, WIDE), (1, 0, 2))
        return total(exchange(out, "front"))[:, :176].astype(BF)


def solution(mesh):
    fronts = mesh.shape["front"]
    grid = Mesh(mesh.devices.reshape(-1, 2, 2, 2, fronts), AXES)
    rows = P(AXES, None)
    in_specs = (P(None, AXES), P(AXES[:4], None)) + (rows,) * 8
    return jax.shard_map(local, mesh=grid, in_specs=in_specs, out_specs=P(None, AXES), check_vma=False)
```
